512 devices in a mesh: dp: 4 (over x), tm: 32 (over y_hi, z), tensor: 4 (over y_lo, core).
Axes of the slice: x: 4, y: 4 (y_hi: 2, y_lo: 2; y = y_hi * 2 + y_lo), z: 16, core: 2. Of those that a mesh axis runs over, the one named last changes fastest.
Arguments:
- tokens: bfloat16 [4, 128, 64, 1536], P('dp', 'tensor', 'tm'), may hold values from -6 to 6
- layer_norm_gain: float32 [1536], replicated, may hold values from 0.1 to 1.9
- query_key_value_weight: bfloat16 [3, 1536, 1536], P(None, 'tm', 'tensor'), may hold values from -4 to 4
- output_projection: bfloat16 [1536, 1536], P('tensor', 'tm'), may hold values from -4 to 4
- adapter_down_maps: bfloat16 [2, 1536, 16], replicated, may hold values from -0.15625 to 0.15625
- adapter_up_maps: bfloat16 [2, 16, 1536], P(None, None, 'tensor'), may hold values from -1.5 to 1.5
- codes: int32 [4], replicated, may hold values from 0 to 1
- offsets: int32 [4], P('dp'), may hold values from 0 to 31
- cotangent: bfloat16 [4, 128, 64, 1536], P('dp', 'tensor', 'tm'), may hold values from -6 to 6
Outputs:
- block_out: bfloat16 [4, 128, 64, 1536], P('dp', 'tensor', 'tm')
- grad_tokens: bfloat16 [4, 128, 64, 1536], P('dp', 'tensor', 'tm')
- grad_down: float32 [2, 1536, 16], replicated
- grad_up: float32 [2, 16, 1536], P(None, None, 'tensor')
The draws below stay inside these ranges and needn't reach their ends.
Inputs may be any that keep to these rules, and one draw needn't show every extreme that they name: `codes`: code 1 marks a projection clipped at twice its columns' root mean square, code 0 one clipped at once that.
All inputs are finite; a program needn't handle non-finite values.
Results may differ from the reference program's by a relative error of at most 0.017.
Values may be sent and summed in bfloat16 or wider, within the bound.
A program may use at most 64 MiB of HBM per device.

```python
import math
import jax
import jax.numpy as jnp
from jax import lax

MODEL_SLICE = 1536
HEADS = 12
HEAD_DIM = 128
ADAPTER_RANK = 16
PATCH = 128
FRAMES = 64
CLIPS = 4
ALL_HEAD_WIDTH = 1536
N_TENSOR = 4


def draw_query_key_value_weight(key, part):
    key = jax.random.fold_in(key, 7)
    key_base, key_rows, key_cols = jax.random.split(key, 3)
    entries = jax.random.truncated_normal(key_base, -3.0, 3.0, (3, MODEL_SLICE, ALL_HEAD_WIDTH), jnp.float32)
    row_scale = jnp.exp(jax.random.uniform(key_rows, (1, MODEL_SLICE, 1), jnp.float32, math.log(0.5), math.log(2.0)))
    col_scale = jnp.exp(jax.random.uniform(key_cols, (3, 1, ALL_HEAD_WIDTH), jnp.float32, math.log(0.5), math.log(2.0)))
    weight = entries * row_scale * col_scale * MODEL_SLICE ** (-0.5)
    return jnp.clip(weight, -4.0, 4.0).astype(jnp.bfloat16)


def draw_output_projection(key, part):
    key = jax.random.fold_in(key, 11)
    key_base, key_rough = jax.random.split(key, 2)
    position = jnp.arange(ALL_HEAD_WIDTH, dtype=jnp.float32)[:, None] / ALL_HEAD_WIDTH
    entries = jax.random.truncated_normal(key_base, -3.0, 3.0, (ALL_HEAD_WIDTH, MODEL_SLICE), jnp.float32)
    rising = jnp.exp(math.log(0.3) + math.log(10.0) * position)
    rough = jnp.exp(jax.random.uniform(key_rough, (ALL_HEAD_WIDTH, 1), jnp.float32, math.log(0.7), math.log(1.4)))
    weight = entries * rising * rough * ALL_HEAD_WIDTH ** (-0.5)
    return jnp.clip(weight, -4.0, 4.0).astype(jnp.bfloat16)


def with_ends(values, stream_key, least, largest):
    longest = values.shape.index(max(values.shape))
    spots = []
    for shift in (0, 1):
        where = [jax.random.randint(jax.random.fold_in(stream_key, axis), (), 0, length) for axis, length in enumerate(values.shape)]
        where[longest] = (where[longest] + shift) % values.shape[longest]
        spots.append(tuple(where))
    return values.at[spots[0]].set(least).at[spots[1]].set(largest)


def block_levels(key, extent, shards, smallest, high):
    def one(axis_at, shards_of):
        heights = jax.random.uniform(jax.random.fold_in(jax.random.fold_in(key, 6), axis_at), (shards_of,), jnp.float32, smallest / len(shards), high / len(shards))
        return jnp.repeat(jnp.exp(heights), extent[axis_at] // shards_of).reshape((-1,) + (1,) * (len(extent) - axis_at - 1))

    loudness = one(*shards[0])
    for cut in shards[1:]:
        loudness = loudness * one(*cut)
    return loudness


def gaussian(rng, dims, scale, limit, cuts=(), kind=jnp.bfloat16):
    factor_of = block_levels(rng, dims, cuts, -0.22, 0.18) if cuts else 1.0
    drawn = jax.random.normal(rng, dims, jnp.float32) * scale * factor_of
    return jnp.minimum(jnp.maximum(drawn, -limit), limit).astype(kind)


def setup_inputs(seed: int = 0) -> dict:
    arg_keys = jax.random.split(jax.random.key(seed), 10)
    return {
        "tokens": gaussian(arg_keys[0], (CLIPS, PATCH, FRAMES, MODEL_SLICE), 1.0, 6.0, ((0, 4), (1, 4), (2, 32))),
        "layer_norm_gain": jnp.clip(1.0 + 0.18 * jax.random.normal(arg_keys[1], (MODEL_SLICE,), jnp.float32), 0.1, 1.9),
        "query_key_value_weight": draw_query_key_value_weight(jax.random.fold_in(arg_keys[9], 71), 0),
        "output_projection": draw_output_projection(jax.random.fold_in(arg_keys[9], 71), 0),
        "adapter_down_maps": gaussian(arg_keys[4], (2, MODEL_SLICE, ADAPTER_RANK), MODEL_SLICE ** -0.5, 0.15625),
        "adapter_up_maps": gaussian(arg_keys[5], (2, ADAPTER_RANK, ALL_HEAD_WIDTH), ADAPTER_RANK ** -0.5, 1.5, ((2, 4),)),
        "codes": with_ends(jax.random.randint(arg_keys[6], (4,), 0, 2), jax.random.fold_in(arg_keys[6], 1), 0, 1).astype(jnp.int32),
        "offsets": with_ends(jax.random.randint(arg_keys[7], (CLIPS,), 0, FRAMES // 2), jax.random.fold_in(arg_keys[7], 1), 0, (FRAMES // 2) - 1).astype(jnp.int32),
        "cotangent": gaussian(arg_keys[8], (CLIPS, PATCH, FRAMES, MODEL_SLICE), 1.0, 6.0, ((0, 4), (1, 4), (2, 32))),
    }


def fake_quant(weight, code):
    wide = weight.astype(jnp.float32)
    mean_sq = lax.optimization_barrier(jnp.mean(wide * wide, axis=0, keepdims=True))
    bound = (1.0 + code.astype(jnp.float32)) * jnp.sqrt(mean_sq + 1e-06)
    return (bound * jnp.tanh(wide / bound)).astype(jnp.bfloat16)

def reference(tokens, layer_norm_gain, query_key_value_weight, output_projection, adapter_down_maps, adapter_up_maps, codes, offsets, cotangent):
    clip_count, patches, frames, model_width = tokens.shape
    row_total = clip_count * patches * frames
    group_width = ALL_HEAD_WIDTH // N_TENSOR
    query_matrix = fake_quant(query_key_value_weight[0], codes[0])
    w_key = fake_quant(query_key_value_weight[1], codes[1])
    value_matrix = fake_quant(query_key_value_weight[2], codes[2])
    w_out = fake_quant(output_projection, codes[3])
    xwide = tokens.astype(jnp.float32).reshape(row_total, model_width)
    mean_row = lax.optimization_barrier(jnp.mean(xwide, axis=1, keepdims=True))
    mean_removed = xwide - mean_row
    variance = lax.optimization_barrier(jnp.mean(mean_removed * mean_removed, axis=1, keepdims=True))
    inverse_deviation = lax.rsqrt(variance + 1e-05)
    standardized = mean_removed * inverse_deviation
    normalized = (standardized * layer_norm_gain[None, :]).astype(jnp.bfloat16)
    query_reduced = jnp.dot(normalized, adapter_down_maps[0], preferred_element_type=jnp.float32).astype(jnp.bfloat16)
    value_reduced = jnp.dot(normalized, adapter_down_maps[1], preferred_element_type=jnp.float32).astype(jnp.bfloat16)
    query_rows_projected = (jnp.dot(normalized, query_matrix, preferred_element_type=jnp.float32) + jnp.dot(query_reduced, adapter_up_maps[0], preferred_element_type=jnp.float32)).astype(jnp.bfloat16)
    keys_proj = jnp.dot(normalized, w_key, preferred_element_type=jnp.float32).astype(jnp.bfloat16)
    value_projected = (jnp.dot(normalized, value_matrix, preferred_element_type=jnp.float32) + jnp.dot(value_reduced, adapter_up_maps[1], preferred_element_type=jnp.float32)).astype(jnp.bfloat16)
    shape_five = (clip_count, patches, frames, HEADS, HEAD_DIM)
    q_five = query_rows_projected.reshape(shape_five).astype(jnp.float32)
    k_five = keys_proj.reshape(shape_five).astype(jnp.float32)
    v_five = value_projected.reshape(shape_five).astype(jnp.float32)
    logit_scale = HEAD_DIM ** (-0.5)
    scores = jnp.einsum('cpthd,cpshd->cphts', q_five, k_five) * logit_scale
    t_index = jnp.arange(frames, dtype=jnp.int32)
    allowed = t_index[None, None, None, None, :] <= t_index[None, None, None, :, None] + offsets[:, None, None, None, None]
    masked = jnp.where(allowed, scores, -1e+30)
    peak = lax.optimization_barrier(jnp.max(masked, axis=-1, keepdims=True))
    expo_terms = jnp.exp(masked - peak)
    prob = expo_terms / lax.optimization_barrier(jnp.sum(expo_terms, axis=-1, keepdims=True))
    prob_b = prob.astype(jnp.bfloat16)
    attended = jnp.einsum('cphts,cpshd->cpthd', prob_b.astype(jnp.float32), v_five).astype(jnp.bfloat16)
    attended_rows = attended.reshape(row_total, ALL_HEAD_WIDTH)
    mixture = jnp.zeros((row_total, model_width), jnp.float32)
    for group in range(N_TENSOR):
        lo_col = group * group_width
        part = jnp.dot(attended_rows[:, lo_col:lo_col + group_width], w_out[lo_col:lo_col + group_width, :], preferred_element_type=jnp.float32).astype(jnp.bfloat16)
        mixture = mixture + part.astype(jnp.float32)
    block_out = (xwide + mixture).astype(jnp.bfloat16).reshape(tokens.shape)
    dy_rows = cotangent.reshape(row_total, model_width)
    d_attended = jnp.dot(dy_rows, w_out.T, preferred_element_type=jnp.float32).astype(jnp.bfloat16)
    do_five = d_attended.reshape(shape_five).astype(jnp.float32)
    att_five = attended.astype(jnp.float32)
    d_prob = jnp.einsum('cpthd,cpshd->cphts', do_five, v_five)
    delta = jnp.einsum('cpthd,cpthd->cpht', do_five, att_five)
    d_score = (prob * (d_prob - delta[..., None])).astype(jnp.bfloat16).astype(jnp.float32)
    d_queries = (jnp.einsum('cphts,cpshd->cpthd', d_score, k_five) * logit_scale).astype(jnp.bfloat16)
    d_keys = (jnp.einsum('cphts,cpthd->cpshd', d_score, q_five) * logit_scale).astype(jnp.bfloat16)
    d_values = jnp.einsum('cphts,cpthd->cpshd', prob_b.astype(jnp.float32), do_five).astype(jnp.bfloat16)
    query_gradient_rows = d_queries.reshape(row_total, ALL_HEAD_WIDTH)
    dk_rows = d_keys.reshape(row_total, ALL_HEAD_WIDTH)
    value_gradient_rows = d_values.reshape(row_total, ALL_HEAD_WIDTH)
    query_low_gradient = jnp.dot(query_gradient_rows, adapter_up_maps[0].T, preferred_element_type=jnp.float32).astype(jnp.bfloat16)
    value_low_gradient = jnp.dot(value_gradient_rows, adapter_up_maps[1].T, preferred_element_type=jnp.float32).astype(jnp.bfloat16)
    grad_down = jnp.stack((jnp.dot(normalized.T, query_low_gradient, preferred_element_type=jnp.float32), jnp.dot(normalized.T, value_low_gradient, preferred_element_type=jnp.float32)))
    grad_up = jnp.stack((jnp.dot(query_reduced.T, query_gradient_rows, preferred_element_type=jnp.float32), jnp.dot(value_reduced.T, value_gradient_rows, preferred_element_type=jnp.float32)))
    normalized_gradient = jnp.zeros((row_total, model_width), jnp.float32)
    for group in range(N_TENSOR):
        lo_col = group * group_width
        cols = slice(lo_col, lo_col + group_width)
        part = jnp.dot(query_gradient_rows[:, cols], query_matrix[:, cols].T, preferred_element_type=jnp.float32) + jnp.dot(dk_rows[:, cols], w_key[:, cols].T, preferred_element_type=jnp.float32) + jnp.dot(value_gradient_rows[:, cols], value_matrix[:, cols].T, preferred_element_type=jnp.float32)
        normalized_gradient = normalized_gradient + part.astype(jnp.bfloat16).astype(jnp.float32)
    normalized_gradient = normalized_gradient + jnp.dot(query_low_gradient, adapter_down_maps[0].T, preferred_element_type=jnp.float32) + jnp.dot(value_low_gradient, adapter_down_maps[1].T, preferred_element_type=jnp.float32)
    gain_applied = normalized_gradient * layer_norm_gain[None, :]
    first_moment = lax.optimization_barrier(jnp.mean(gain_applied, axis=1, keepdims=True))
    second_moment = lax.optimization_barrier(jnp.mean(gain_applied * standardized, axis=1, keepdims=True))
    input_gradient = inverse_deviation * (gain_applied - first_moment - standardized * second_moment)
    grad_tokens = (dy_rows.astype(jnp.float32) + input_gradient).astype(jnp.bfloat16).reshape(tokens.shape)
    return (block_out, grad_tokens, grad_down, grad_up)
```

```python
import jax
import jax.numpy as jnp
from jax import lax
from jax.sharding import PartitionSpec as P

HEAD_DIM = 128
F32 = jnp.float32
BF16 = jnp.bfloat16


def quantize(wide, sq_sum, count, code):
    bound = (1.0 + code.astype(F32)) * jnp.sqrt(sq_sum / count + 1e-06)
    return (bound * jnp.tanh(wide / bound)).astype(BF16)


def standardize(rows):
    wide = rows.astype(F32)
    removed = wide - jnp.mean(wide, axis=-1, keepdims=True)
    rstd = lax.rsqrt(jnp.mean(removed * removed, axis=-1, keepdims=True) + 1e-05)
    return removed * rstd, rstd


def dot(spec, a, b):
    return jnp.einsum(spec, a, b, preferred_element_type=F32)


def local_block(tok_all, cot_all, gain, qkv, out_t, down, up, codes, offset):
    patches, frames, width = tok_all.shape
    heads_width = qkv.shape[2]
    wide = qkv.astype(F32)
    weights = quantize(wide, jnp.sum(wide * wide, axis=1, keepdims=True), width, codes[0:3][:, None, None])
    xhat, _ = standardize(tok_all.reshape(-1, width))
    normed = (xhat * gain).astype(BF16)
    low = dot("rd,kde->kre", normed, down).astype(BF16)
    lift = dot("kre,kec->krc", low, up)
    proj = dot("rd,kdc->krc", normed, weights)
    split = (patches, frames, heads_width // HEAD_DIM, HEAD_DIM)
    q = (proj[0] + lift[0]).astype(BF16).reshape(split)
    k = proj[1].astype(BF16).reshape(split)
    v = (proj[2] + lift[1]).astype(BF16).reshape(split)
    scale = HEAD_DIM ** (-0.5)
    scores = dot("pthd,pshd->phts", q, k) * scale
    t_at = lax.broadcasted_iota(jnp.int32, (frames, frames), 0)
    s_at = lax.broadcasted_iota(jnp.int32, (frames, frames), 1)
    masked = jnp.where((s_at <= t_at + offset)[None, None], scores, -1e30)
    expo = jnp.exp(masked - jnp.max(masked, axis=-1, keepdims=True))
    prob = expo / jnp.sum(expo, axis=-1, keepdims=True)
    prob_b = prob.astype(BF16)
    att = dot("phts,pshd->pthd", prob_b, v).astype(BF16)
    mixture = dot("rc,dc->rd", att.reshape(-1, heads_width), out_t).astype(BF16)
    d_att = dot("rd,dc->rc", cot_all.reshape(-1, width), out_t).astype(BF16).reshape(split)
    d_prob = dot("pthd,pshd->phts", d_att, v)
    delta = dot("pthd,pthd->pht", d_att, att)
    d_score = (prob * (d_prob - delta[..., None])).astype(BF16)
    dq = (dot("phts,pshd->pthd", d_score, k) * scale).astype(BF16).reshape(-1, heads_width)
    dk = (dot("phts,pthd->pshd", d_score, q) * scale).astype(BF16).reshape(-1, heads_width)
    dv = dot("phts,pthd->pshd", prob_b, d_att).astype(BF16).reshape(-1, heads_width)
    d_out = jnp.stack((dq, dv))
    d_low = dot("krc,kec->kre", d_out, up).astype(BF16)
    d_normed = (
        dot("krc,kdc->rd", jnp.stack((dq, dk, dv)), weights) + dot("kre,kde->rd", d_low, down)
    ).astype(BF16)
    down_part = dot("kre,rd->ked", d_low, normed)
    up_part = dot("kre,krc->kec", low, d_out)
    return mixture, d_normed, down_part, up_part


def on_device(tokens, gain, qkv, out, down, up, codes, offsets, cotangent):
    n_tensor = lax.axis_size("tensor")
    own = lax.axis_index("tensor")
    out_wide = out.astype(F32)
    out_sq = lax.psum(jnp.sum(out_wide * out_wide, axis=0), "tensor")
    out_quant = quantize(out_wide, out_sq[None, :], out.shape[0] * n_tensor, codes[3])
    shard = jnp.concatenate((qkv, out_quant.T[None]))
    full = lax.all_gather(shard, "tm", axis=1, tiled=True)
    both = jnp.stack((tokens[0], cotangent[0]))
    swapped = lax.all_to_all(both, "tm", split_axis=1, concat_axis=2, tiled=True)[:, 0]
    everyone = lax.all_gather(swapped, "tensor", axis=1, tiled=False)
    wide_all, rows = everyone.shape[1], everyone.shape[2]
    mixture, d_normed, down_part, up_part = local_block(
        everyone[0], everyone[1], gain, full[0:3], full[3], down, up, codes, offsets[0]
    )
    width = tokens.shape[-1]
    parts = jnp.stack((mixture, d_normed)).reshape(2, n_tensor, rows, width)
    sums = lax.psum_scatter(parts, "tensor", scatter_dimension=1, tiled=False).astype(F32)
    rank = down.shape[2]
    heads_width = qkv.shape[2]
    down_mine = lax.psum_scatter(
        down_part.reshape(2 * rank, n_tensor, width // n_tensor), "tensor", scatter_dimension=1, tiled=False
    )
    grads = lax.psum(jnp.concatenate((down_mine, up_part.reshape(2 * rank, heads_width))), ("dp", "tm"))
    grad_up = grads[2 * rank :].reshape(up.shape)
    grad_down = lax.all_gather(grads[: 2 * rank], "tensor", axis=1, tiled=True)
    grad_down = grad_down.reshape(2, rank, width).transpose(0, 2, 1)
    xhat, rstd = standardize(swapped[0])
    block_out = (swapped[0].astype(F32) + sums[0]).astype(BF16)
    g = sums[1] * gain
    m1 = jnp.mean(g, axis=-1, keepdims=True)
    m2 = jnp.mean(g * xhat, axis=-1, keepdims=True)
    grad_tokens = (swapped[1].astype(F32) + rstd * (g - m1 - xhat * m2)).astype(BF16)
    back = jnp.stack((block_out, grad_tokens))[:, None]
    back = lax.all_to_all(back, "tm", split_axis=2, concat_axis=1, tiled=True)
    return back[0][None], back[1][None], grad_down, grad_up


def solution(mesh):
    return jax.shard_map(
        on_device,
        mesh=mesh,
        in_specs=(
            P("dp", "tensor", "tm", None),
            P(),
            P(None, "tm", "tensor"),
            P("tensor", "tm"),
            P(),
            P(None, None, "tensor"),
            P(),
            P("dp"),
            P("dp", "tensor", "tm", None),
        ),
        out_specs=(
            P("dp", "tensor", "tm", None),
            P("dp", "tensor", "tm", None),
            P(),
            P(None, None, "tensor"),
        ),
        check_vma=False,
    )
```

```python
import functools

import jax
import jax.numpy as jnp
from jax import lax
from jax.experimental import pallas as pl
from jax.experimental.pallas import tpu as pltpu
from jax.sharding import PartitionSpec as P

MESH = pl.DeviceIdType.MESH
ANY = pl.BlockSpec(memory_space=pl.ANY)
VMEM = pl.BlockSpec(memory_space=pltpu.VMEM)
DMA = pltpu.SemaphoreType.DMA
Z = 16

HEAD_DIM = 128
F32 = jnp.float32
BF16 = jnp.bfloat16


def quantize(wide, sq_sum, count, code):
    bound = (1.0 + code.astype(F32)) * jnp.sqrt(sq_sum / count + 1e-06)
    return (bound * jnp.tanh(wide / bound)).astype(BF16)


def standardize(rows):
    wide = rows.astype(F32)
    removed = wide - jnp.mean(wide, axis=-1, keepdims=True)
    rstd = lax.rsqrt(jnp.mean(removed * removed, axis=-1, keepdims=True) + 1e-05)
    return removed * rstd, rstd


def dot(spec, a, b):
    return jnp.einsum(spec, a, b, preferred_element_type=F32)


def local_block(tok_all, cot_all, gain, qkv, out_t, down, up, codes, offset):
    patches, frames, width = tok_all.shape
    heads_width = qkv.shape[2]
    wide = qkv.astype(F32)
    weights = quantize(wide, jnp.sum(wide * wide, axis=1, keepdims=True), width, codes[0:3][:, None, None])
    xhat, _ = standardize(tok_all.reshape(-1, width))
    normed = (xhat * gain).astype(BF16)
    low = dot("rd,kde->kre", normed, down).astype(BF16)
    lift = dot("kre,kec->krc", low, up)
    proj = dot("rd,kdc->krc", normed, weights)
    split = (patches, frames, heads_width // HEAD_DIM, HEAD_DIM)
    q = (proj[0] + lift[0]).astype(BF16).reshape(split)
    k = proj[1].astype(BF16).reshape(split)
    v = (proj[2] + lift[1]).astype(BF16).reshape(split)
    scale = HEAD_DIM ** (-0.5)
    scores = dot("pthd,pshd->phts", q, k) * scale
    t_at = lax.broadcasted_iota(jnp.int32, (frames, frames), 0)
    s_at = lax.broadcasted_iota(jnp.int32, (frames, frames), 1)
    masked = jnp.where((s_at <= t_at + offset)[None, None], scores, -1e30)
    expo = jnp.exp(masked - jnp.max(masked, axis=-1, keepdims=True))
    prob = expo / jnp.sum(expo, axis=-1, keepdims=True)
    prob_b = prob.astype(BF16)
    att = dot("phts,pshd->pthd", prob_b, v).astype(BF16)
    mixture = dot("rc,dc->rd", att.reshape(-1, heads_width), out_t).astype(BF16)
    d_att = dot("rd,dc->rc", cot_all.reshape(-1, width), out_t).astype(BF16).reshape(split)
    d_prob = dot("pthd,pshd->phts", d_att, v)
    delta = dot("pthd,pthd->pht", d_att, att)
    d_score = (prob * (d_prob - delta[..., None])).astype(BF16)
    dq = (dot("phts,pshd->pthd", d_score, k) * scale).astype(BF16).reshape(-1, heads_width)
    dk = (dot("phts,pthd->pshd", d_score, q) * scale).astype(BF16).reshape(-1, heads_width)
    dv = dot("phts,pthd->pshd", prob_b, d_att).astype(BF16).reshape(-1, heads_width)
    d_out = jnp.stack((dq, dv))
    d_low = dot("krc,kec->kre", d_out, up).astype(BF16)
    d_normed = (
        dot("krc,kdc->rd", jnp.stack((dq, dk, dv)), weights) + dot("kre,kde->rd", d_low, down)
    ).astype(BF16)
    down_part = dot("kre,rd->ked", d_low, normed)
    up_part = dot("kre,krc->kec", low, d_out)
    return mixture, d_normed, down_part, up_part


def remote(src, dst, send, recv, **where):
    return pltpu.make_async_remote_copy(
        src_ref=src, dst_ref=dst, send_sem=send, recv_sem=recv, device_id=where, device_id_type=MESH
    )


def await_bytes(ref, sem):
    pltpu.make_async_copy(ref, ref, sem).wait()


def greet(signals):
    barrier = pltpu.get_barrier_semaphore()
    total = 0
    for axis_of, count in signals:

        def one(step, carry, axis_of=axis_of):
            pl.semaphore_signal(barrier, inc=1, device_id=axis_of(step), device_id_type=MESH)
            return carry

        lax.fori_loop(1, count + 1, one, 0)
        total += count
    pl.semaphore_wait(barrier, total)


def gather_kernel(
    n_dp, n_tm, n_tensor, tok, cot, shard, all_tok, all_cot, w,
    swap_send, swap_recv, spread_send, spread_recv,
    z_send, z_recv, y_send, y_recv, x_send, x_recv, local,
):
    x, tm, t = lax.axis_index("dp"), lax.axis_index("tm"), lax.axis_index("tensor")
    z, yh = tm % Z, tm // Z
    up_z = yh * Z + (z + 1) % Z
    down_z = yh * Z + (z + Z - 1) % Z
    other = (tm + Z) % n_tm
    greet(
        (
            (lambda d: {"tm": (tm + d) % n_tm}, n_tm - 1),
            (lambda d: {"tensor": (t + d) % n_tensor}, n_tensor - 1),
            (lambda d: {"dp": (x + 2 * d + 3) % n_dp}, 2),
        )
    )
    mats = (x, (x + 2) % n_dp)

    def to_z(src, i, piece, half, zs, step, up):
        m = mats[i]
        side = 0 if up else 1
        remote(
            src, w.at[m, half, zs], z_send.at[side], z_recv.at[side, step, piece],
            tm=up_z if up else down_z,
        ).start()

    def to_x(src, half, zs):
        for side, dest in ((0, (x + 1) % n_dp), (1, (x + n_dp - 1) % n_dp)):
            remote(src, w.at[x, half, zs], x_send.at[side], x_recv.at[side], dp=dest).start()

    for i in range(2):
        remote(shard.at[mats[i]], w.at[mats[i], yh, z], y_send, y_recv.at[i], tm=other).start()
    for i in range(2):
        to_z(shard.at[mats[i]], i, i, yh, z, 0, True)
        to_z(shard.at[mats[i]], i, i, yh, z, 0, False)
    to_x(shard.at[x], yh, z)
    for i in range(2):
        pltpu.make_async_copy(shard.at[mats[i]], w.at[mats[i], yh, z], local).start()

    for k, (src, dst) in enumerate(((tok, all_tok), (cot, all_cot))):
        pltpu.make_async_copy(src.at[tm], dst.at[t, tm], swap_recv.at[k]).start()

        def send_one(d, carry, src=src, dst=dst, k=k):
            peer = (tm + d) % n_tm
            remote(src.at[peer], dst.at[t, tm], swap_send.at[k], swap_recv.at[k], tm=peer).start()
            return carry

        lax.fori_loop(1, n_tm, send_one, 0)

    for i in range(2):
        here = w.at[mats[i], 1 - yh, z]
        await_bytes(here, y_recv.at[i])
        to_z(here, i, 2 + i, 1 - yh, z, 0, True)
        to_z(here, i, 2 + i, 1 - yh, z, 0, False)
        if i == 0:
            to_x(here, 1 - yh, z)

    def arrive(step, up, onward):
        zs = (z + Z - 1 - step) % Z if up else (z + 1 + step) % Z
        side = 0 if up else 1
        for piece in range(4):
            i = piece % 2
            half = yh if piece < 2 else 1 - yh
            here = w.at[mats[i], half, zs]
            await_bytes(here, z_recv.at[side, step, piece])
            if onward:
                to_z(here, i, piece, half, zs, step + 1, up)
            if i == 0:
                to_x(here, half, zs)

    def ring(step, carry):
        arrive(step, True, True)
        arrive(step, False, True)
        return carry

    lax.fori_loop(0, Z // 2 - 2, ring, 0)
    arrive(Z // 2 - 2, True, True)
    arrive(Z // 2 - 2, False, False)
    arrive(Z // 2 - 1, True, False)

    for k, dst in ((0, all_tok), (1, all_cot)):
        await_bytes(dst.at[t], swap_recv.at[k])
        for d in range(1, n_tensor):
            remote(
                dst.at[t], dst.at[t], spread_send.at[k], spread_recv.at[k], tensor=(t + d) % n_tensor
            ).start()
    for k, (src, dst) in enumerate(((tok, all_tok), (cot, all_cot))):
        await_bytes(src.at[pl.ds(0, n_tm - 1)], swap_send.at[k])
        await_bytes(dst.at[pl.ds(0, n_tensor - 1)], spread_send.at[k])
        await_bytes(dst.at[pl.ds(0, n_tensor - 1)], spread_recv.at[k])
    await_bytes(w.at[0, 0, pl.ds(0, 2)], local)
    await_bytes(w.at[0, 0, pl.ds(0, 2)], y_send)
    await_bytes(w.at[0], z_send.at[0])
    await_bytes(w.at[0, :, pl.ds(0, Z - 2)], z_send.at[1])
    await_bytes(w.at[(x + n_dp - 1) % n_dp], x_recv.at[0])
    await_bytes(w.at[(x + 1) % n_dp], x_recv.at[1])
    await_bytes(w.at[0], x_send.at[0])
    await_bytes(w.at[0], x_send.at[1])


def gather(tok, cot, shard, sizes):
    n_dp, n_tm, n_tensor = sizes
    everyone = jax.ShapeDtypeStruct((n_tensor,) + tok.shape, BF16)
    return pl.pallas_call(
        functools.partial(gather_kernel, n_dp, n_tm, n_tensor),
        out_shape=(
            everyone,
            everyone,
            jax.ShapeDtypeStruct((4, n_tm // Z, Z) + shard.shape[1:], BF16),
        ),
        in_specs=[ANY] * 3,
        out_specs=(ANY,) * 3,
        scratch_shapes=[
            DMA((2,)), DMA((2,)), DMA((2,)), DMA((2,)),
            DMA((2,)), DMA((2, Z // 2, 4)), DMA, DMA((2,)), DMA((2,)), DMA((2,)), DMA,
        ],
        compiler_params=pltpu.CompilerParams(collective_id=0, has_side_effects=True),
    )(tok, cot, shard)


def scatter_kernel(n_tensor, *refs):
    ins, outs = refs[0:3], refs[3:6]
    send, recv = refs[6:8]
    t = lax.axis_index("tensor")
    greet(((lambda d: {"tensor": (t + d) % n_tensor}, n_tensor - 1),))
    for k in range(3):
        for d in range(1, n_tensor):
            peer = (t + d) % n_tensor
            remote(ins[k].at[peer], outs[k].at[t], send.at[k], recv.at[k], tensor=peer).start()
        pltpu.make_async_copy(ins[k].at[t], outs[k].at[t], recv.at[k]).start()
    for k in range(3):
        await_bytes(outs[k], recv.at[k])
        await_bytes(outs[k].at[pl.ds(0, n_tensor - 1)], send.at[k])


def scatter(parts, n_tensor):
    return pl.pallas_call(
        functools.partial(scatter_kernel, n_tensor),
        out_shape=tuple(jax.ShapeDtypeStruct(p.shape, p.dtype) for p in parts),
        in_specs=[ANY] * 3,
        out_specs=(ANY,) * 3,
        scratch_shapes=[DMA((3,)), DMA((3,))],
        compiler_params=pltpu.CompilerParams(collective_id=1, has_side_effects=True),
    )(*parts)


def return_kernel(
    n_dp, n_tm, n_tensor, out, grad, part, out_back, grad_back, total, down_all,
    first, second, mine, swap_send, swap_recv, g_send, g_recv,
):
    x, tm, t = lax.axis_index("dp"), lax.axis_index("tm"), lax.axis_index("tensor")
    z, yh = tm % Z, tm // Z
    n_half = n_tm // Z
    n_group = n_dp * n_half
    r = x * n_half + yh
    greet(
        (
            (lambda d: {"tm": (tm + d) % n_tm}, n_tm - 1),
            (lambda d: {"tensor": (t + d) % n_tensor}, n_tensor - 1),
            (lambda d: {"dp": (x + d) % n_dp}, n_dp - 1),
            (lambda d: {"dp": (x + d) % n_dp, "tm": (tm + Z) % n_tm}, n_dp - 1),
        )
    )

    def to_group(pick, dst, stage):
        def one(d, carry):
            peer = (r + d) % n_group
            remote(
                pick(peer), dst.at[r], g_send.at[stage], g_recv.at[stage],
                dp=peer // n_half, tm=(peer % n_half) * Z + z,
            ).start()
            return carry

        lax.fori_loop(1, n_group, one, 0)

    to_group(lambda peer: part.at[peer], first, 0)
    for k, (src, dst) in enumerate(((out, out_back), (grad, grad_back))):
        pltpu.make_async_copy(src.at[tm], dst.at[tm], swap_recv.at[k]).start()

        def send_one(d, carry, src=src, dst=dst, k=k):
            peer = (tm + d) % n_tm
            remote(src.at[peer], dst.at[tm], swap_send.at[k], swap_recv.at[k], tm=peer).start()
            return carry

        lax.fori_loop(1, n_tm, send_one, 0)
    first[r] = part[r]
    await_bytes(first.at[pl.ds(0, n_group - 1)], g_recv.at[0])
    mine[0] = jnp.sum(first[...], axis=0)
    second[z] = mine[0]

    def along_z(d, carry):
        peer = (z + d) % Z
        remote(mine.at[0], second.at[z], g_send.at[1], g_recv.at[1], tm=yh * Z + peer).start()
        return carry

    lax.fori_loop(1, Z, along_z, 0)
    await_bytes(second.at[pl.ds(0, Z - 1)], g_recv.at[1])
    mine[1] = jnp.sum(second[...], axis=0)
    total[r] = mine[1]
    to_group(lambda peer: mine.at[1], total, 2)
    await_bytes(total.at[pl.ds(0, n_group - 1)], g_recv.at[2])
    half = pl.ds(0, n_group // 2)
    for d in range(1, n_tensor):
        remote(
            total.at[half], down_all.at[t], g_send.at[3], g_recv.at[3], tensor=(t + d) % n_tensor
        ).start()
    down_all[t] = total[half]
    await_bytes(down_all.at[pl.ds(0, n_tensor - 1)], g_recv.at[3])
    await_bytes(first.at[pl.ds(0, n_group - 1)], g_send.at[0])
    await_bytes(second.at[pl.ds(0, Z - 1)], g_send.at[1])
    await_bytes(first.at[pl.ds(0, n_group - 1)], g_send.at[2])
    await_bytes(down_all.at[pl.ds(0, n_tensor - 1)], g_send.at[3])
    for k, (src, dst) in enumerate(((out, out_back), (grad, grad_back))):
        await_bytes(dst, swap_recv.at[k])
        await_bytes(src.at[pl.ds(0, n_tm - 1)], swap_send.at[k])


def send_back(out, grad, part, sizes):
    n_dp, n_tm, n_tensor = sizes
    n_group = part.shape[0]
    chunk = part.shape[1:]
    same = jax.ShapeDtypeStruct(out.shape, BF16)
    return pl.pallas_call(
        functools.partial(return_kernel, n_dp, n_tm, n_tensor),
        out_shape=(
            same,
            same,
            jax.ShapeDtypeStruct(part.shape, F32),
            jax.ShapeDtypeStruct((n_tensor, n_group // 2) + chunk, F32),
        ),
        in_specs=[ANY, ANY, VMEM],
        out_specs=(ANY, ANY, VMEM, VMEM),
        scratch_shapes=[
            pltpu.VMEM(part.shape, F32),
            pltpu.VMEM((Z,) + chunk, F32),
            pltpu.VMEM((2,) + chunk, F32),
            DMA((2,)), DMA((2,)), DMA((4,)), DMA((4,)),
        ],
        compiler_params=pltpu.CompilerParams(collective_id=2, has_side_effects=True),
    )(out, grad, part)


def on_device(tokens, gain, qkv, out, down, up, codes, offsets, cotangent):
    sizes = tuple(lax.axis_size(a) for a in ("dp", "tm", "tensor"))
    n_dp, n_tm, n_tensor = sizes
    own = lax.axis_index("tensor")
    width = tokens.shape[-1]
    rank, heads_width = down.shape[2], qkv.shape[2]
    out_wide = out.astype(F32)
    out_sq = lax.psum(jnp.sum(out_wide * out_wide, axis=0), "tensor")
    out_quant = quantize(out_wide, out_sq[None, :], out.shape[0] * n_tensor, codes[3])
    shard = jnp.concatenate((qkv, out_quant.T[None]))
    all_tok, all_cot, full = gather(tokens[0], cotangent[0], shard, sizes)
    full = full.reshape(4, width, heads_width)
    tok_all = all_tok.reshape(n_tensor, -1, width)
    cot_all = all_cot.reshape(n_tensor, -1, width)
    mixture, d_normed, down_part, up_part = local_block(
        tok_all, cot_all, gain, full[0:3], full[3], down, up, codes, offsets[0]
    )
    rows = tok_all.shape[1]
    down_part = down_part.reshape(2 * rank, n_tensor, heads_width).transpose(1, 0, 2)
    mix_parts, normed_parts, down_parts = scatter(
        (
            mixture.reshape(n_tensor, rows, width),
            d_normed.reshape(n_tensor, rows, width),
            down_part,
        ),
        n_tensor,
    )
    n_group = n_dp * n_tm // Z
    part = jnp.stack((jnp.sum(down_parts, axis=0), up_part.reshape(2 * rank, heads_width)))
    part = part.reshape(n_group, -1, 128)
    tok_own = lax.dynamic_index_in_dim(tok_all, own, keepdims=False)
    cot_own = lax.dynamic_index_in_dim(cot_all, own, keepdims=False)
    xhat, rstd = standardize(tok_own)
    block_out = (tok_own.astype(F32) + jnp.sum(mix_parts.astype(F32), axis=0)).astype(BF16)
    g = jnp.sum(normed_parts.astype(F32), axis=0) * gain
    m1 = jnp.mean(g, axis=-1, keepdims=True)
    m2 = jnp.mean(g * xhat, axis=-1, keepdims=True)
    grad_tokens = (cot_own.astype(F32) + rstd * (g - m1 - xhat * m2)).astype(BF16)
    shape = tokens.shape[1:]
    block_out, grad_tokens, total, down_all = send_back(
        block_out.reshape(shape), grad_tokens.reshape(shape), part, sizes
    )
    grad_up = total.reshape(2, 2, rank, heads_width)[1]
    grad_down = down_all.reshape(n_tensor, 2, rank, heads_width).transpose(1, 0, 3, 2)
    return block_out[None], grad_tokens[None], grad_down.reshape(2, width, rank), grad_up


def solution(mesh):
    return jax.shard_map(
        on_device,
        mesh=mesh,
        in_specs=(
            P("dp", "tensor", "tm", None),
            P(),
            P(None, "tm", "tensor"),
            P("tensor", "tm"),
            P(),
            P(None, None, "tensor"),
            P(),
            P("dp"),
            P("dp", "tensor", "tm", None),
        ),
        out_specs=(
            P("dp", "tensor", "tm", None),
            P("dp", "tensor", "tm", None),
            P(),
            P(None, None, "tensor"),
        ),
        check_vma=False,
    )
```

```python
import functools

import jax
import jax.numpy as jnp
from jax import lax
from jax.experimental import pallas as pl
from jax.experimental.pallas import tpu as pltpu
from jax.sharding import PartitionSpec as P

MESH = pl.DeviceIdType.MESH
ANY = pl.BlockSpec(memory_space=pl.ANY)
VMEM = pl.BlockSpec(memory_space=pltpu.VMEM)
SMEM = pl.BlockSpec(memory_space=pltpu.SMEM)
DMA = pltpu.SemaphoreType.DMA
Z = 16
CHUNK = 16

HEAD_DIM = 128
F32 = jnp.float32
BF16 = jnp.bfloat16


def standardize(rows):
    wide = rows.astype(F32)
    removed = wide - jnp.mean(wide, axis=-1, keepdims=True)
    rstd = lax.rsqrt(jnp.mean(removed * removed, axis=-1, keepdims=True) + 1e-05)
    return removed * rstd, rstd


def remote(src, dst, send, recv, **where):
    return pltpu.make_async_remote_copy(
        src_ref=src, dst_ref=dst, send_sem=send, recv_sem=recv, device_id=where, device_id_type=MESH
    )


def await_bytes(ref, sem):
    pltpu.make_async_copy(ref, ref, sem).wait()


def greet(signals):
    barrier = pltpu.get_barrier_semaphore()
    total = 0
    for axis_of, count in signals:

        def one(step, carry, axis_of=axis_of):
            pl.semaphore_signal(barrier, inc=1, device_id=axis_of(step), device_id_type=MESH)
            return carry

        lax.fori_loop(1, count + 1, one, 0)
        total += count
    pl.semaphore_wait(barrier, total)


def gather_kernel(
    n_dp, n_tm, n_tensor, codes, tok, cot, qkv, out_t, all_tok, all_cot, w,
    shard, sq, landed, flat, sq_send, sq_recv, swap_send, swap_recv, spread_send, far_recv, near_recv, own,
    z_send, z_recv, y_send, y_first, y_recv, x_send, x_recv, local,
):
    x, tm, t = lax.axis_index("dp"), lax.axis_index("tm"), lax.axis_index("tensor")
    z, yh = tm % Z, tm // Z
    up_z = yh * Z + (z + 1) % Z
    down_z = yh * Z + (z + Z - 1) % Z
    other = (tm + Z) % n_tm
    near = t + 1 - 2 * (t % 2)
    far = (t + 2) % n_tensor
    mats = (x, (x + 2) % n_dp)
    greet(
        (
            (lambda d: {"tm": (tm + d) % n_tm}, n_tm - 1),
            (lambda d: {"tensor": (t + d) % n_tensor}, n_tensor - 1),
            (lambda d: {"dp": (x + 2 * d + 3) % n_dp}, 2),
        )
    )
    wide = out_t[...].astype(F32)
    sq[t] = jnp.broadcast_to(jnp.sum(wide * wide, axis=1, keepdims=True), sq.shape[1:])
    for d in range(1, n_tensor):
        remote(sq.at[t], sq.at[t], sq_send, sq_recv, tensor=(t + d) % n_tensor).start()
    for j in range(3):
        shard[j] = qkv[j]
    for k, src in enumerate((tok, cot)):
        pltpu.make_async_copy(src.at[tm], landed.at[k, tm], swap_recv.at[k]).start()

        def send_one(d, carry, src=src, k=k):
            peer = (tm + d) % n_tm
            remote(
                src.at[peer], landed.at[k, tm], swap_send.at[k], swap_recv.at[k], tm=peer
            ).start()
            return carry

        lax.fori_loop(1, n_tm, send_one, 0)
    await_bytes(sq.at[pl.ds(0, n_tensor - 1)], sq_recv)
    await_bytes(sq.at[pl.ds(0, n_tensor - 1)], sq_send)
    mean_sq = jnp.sum(sq[...], axis=0)[:, 0:1] / (n_tensor * out_t.shape[1])
    bound = (1.0 + codes[3].astype(F32)) * jnp.sqrt(mean_sq + 1e-06)
    shard[3] = (bound * jnp.tanh(wide / bound)).astype(BF16)

    def to_z(src, i, piece, half, zs, step, up):
        side = 0 if up else 1
        remote(
            src, w.at[mats[i], half, zs], z_send.at[side], z_recv.at[side, step, piece],
            tm=up_z if up else down_z,
        ).start()

    def to_x(src, half, zs):
        for side, dest in ((0, (x + 1) % n_dp), (1, (x + n_dp - 1) % n_dp)):
            remote(src, w.at[x, half, zs], x_send.at[side], x_recv.at[side], dp=dest).start()

    def to_y(src, zs):
        remote(src, w.at[mats[1], yh, zs], y_send, y_recv, tm=other).start()

    remote(shard.at[x], w.at[x, yh, z], y_send, y_first, tm=other).start()
    for i in range(2):
        to_z(shard.at[mats[i]], i, i, yh, z, 0, True)
        to_z(shard.at[mats[i]], i, i, yh, z, 0, False)
    to_x(shard.at[x], yh, z)
    to_y(shard.at[mats[1]], z)
    for i in range(2):
        pltpu.make_async_copy(shard.at[mats[i]], w.at[mats[i], yh, z], local).start()
    here = w.at[x, 1 - yh, z]
    await_bytes(here, y_first)
    to_z(here, 0, 2, 1 - yh, z, 0, True)
    to_z(here, 0, 2, 1 - yh, z, 0, False)
    to_x(here, 1 - yh, z)

    def arrive(step, up, onward):
        zs = (z + Z - 1 - step) % Z if up else (z + 1 + step) % Z
        side = 0 if up else 1
        for piece, (i, half) in enumerate(((0, yh), (1, yh), (0, 1 - yh))):
            here = w.at[mats[i], half, zs]
            await_bytes(here, z_recv.at[side, step, piece])
            if onward:
                to_z(here, i, piece, half, zs, step + 1, up)
            if i == 0:
                to_x(here, half, zs)
            else:
                to_y(here, zs)

    def ring(step, carry):
        arrive(step, True, True)
        arrive(step, False, True)
        return carry

    outs = (all_tok, all_cot)

    def spread(k):
        await_bytes(landed.at[k], swap_recv.at[k])
        for i in range(flat.shape[1] // CHUNK):
            pairs = landed[k, i * CHUNK // 2 : (i + 1) * CHUNK // 2].astype(F32)
            flat[k, i * CHUNK : (i + 1) * CHUNK, :] = pairs.reshape(CHUNK, -1).astype(BF16)
        remote(flat.at[k], outs[k].at[t], spread_send.at[k], far_recv.at[k], tensor=far).start()
        remote(flat.at[k], outs[k].at[t], spread_send.at[k], near_recv.at[k], tensor=near).start()
        pltpu.make_async_copy(flat.at[k], outs[k].at[t], own).start()

    def forward(k):
        await_bytes(outs[k].at[far], far_recv.at[k])
        remote(
            outs[k].at[far], outs[k].at[far], spread_send.at[k], near_recv.at[k], tensor=near
        ).start()

    half_way = 4
    lax.fori_loop(0, half_way, ring, 0)
    spread(0)
    spread(1)
    lax.fori_loop(half_way, Z // 2 - 2, ring, 0)
    arrive(Z // 2 - 2, True, True)
    arrive(Z // 2 - 2, False, False)
    arrive(Z // 2 - 1, True, False)
    forward(0)
    forward(1)
    for k, dst in enumerate(outs):
        await_bytes(dst.at[pl.ds(0, 2)], near_recv.at[k])
        await_bytes(dst.at[pl.ds(0, 3)], spread_send.at[k])
        await_bytes(landed.at[k, pl.ds(0, n_tm - 1)], swap_send.at[k])
    await_bytes(all_tok.at[pl.ds(0, 2)], own)
    await_bytes(w.at[0, 0, pl.ds(0, 2)], local)
    await_bytes(w.at[mats[1], 1 - yh], y_recv)
    await_bytes(w.at[0, 0, pl.ds(0, 1)], y_send)
    await_bytes(w.at[0, 0], y_send)
    for j in range(3):
        await_bytes(w.at[0, 0, pl.ds(0, Z // 2)], z_send.at[0])
        await_bytes(w.at[0, 0, pl.ds(0, Z // 2 - 1)], z_send.at[1])
    await_bytes(w.at[(x + n_dp - 1) % n_dp], x_recv.at[0])
    await_bytes(w.at[(x + 1) % n_dp], x_recv.at[1])
    await_bytes(w.at[0], x_send.at[0])
    await_bytes(w.at[0], x_send.at[1])


def gather(tok, cot, qkv, out_t, codes, sizes):
    n_dp, n_tm, n_tensor = sizes
    patches, few, width = tok.shape
    rows = patches * few
    everyone = jax.ShapeDtypeStruct((n_tensor, rows, width), BF16)
    return pl.pallas_call(
        functools.partial(gather_kernel, n_dp, n_tm, n_tensor),
        out_shape=(
            everyone,
            everyone,
            jax.ShapeDtypeStruct((4, n_tm // Z, Z) + qkv.shape[1:], BF16),
        ),
        in_specs=[SMEM, ANY, ANY, VMEM, VMEM],
        out_specs=(ANY,) * 3,
        scratch_shapes=[
            pltpu.VMEM((4,) + qkv.shape[1:], BF16),
            pltpu.VMEM((n_tensor, out_t.shape[0], 128), F32),
            pltpu.VMEM((2,) + tok.shape, BF16),
            pltpu.VMEM((2, rows, width), BF16),
            DMA, DMA, DMA((2,)), DMA((2,)), DMA((2,)), DMA((2,)), DMA((2,)), DMA,
            DMA((2,)), DMA((2, Z // 2, 3)), DMA, DMA, DMA, DMA((2,)), DMA((2,)), DMA,
        ],
        compiler_params=pltpu.CompilerParams(
            collective_id=0, has_side_effects=True, vmem_limit_bytes=32 << 20
        ),
    )(codes, tok, cot, qkv, out_t)


def nn(a, b):
    return jnp.dot(a, b, preferred_element_type=F32)


def nt(a, b):
    return lax.dot_general(a, b, (((1,), (1,)), ((), ())), preferred_element_type=F32)


def tn(a, b):
    return lax.dot_general(a, b, (((0,), (0,)), ((), ())), preferred_element_type=F32)


def block_kernel(
    frames, codes, offsets, tok, cot, w, gain, down, up, mixture, d_normed, down_part, up_part,
    weights, normed, q, k, v, att, d_att, grads, low,
):
    rows, width = normed.shape
    heads_width = q.shape[1]
    rank = up.shape[1]
    n_patch = rows // frames
    deep = 192

    for j in range(3):

        def squares(i, total, j=j):
            wide = w[j, pl.ds(pl.multiple_of(i * deep, deep), deep), :].astype(F32)
            return total + jnp.sum((wide * wide).reshape(deep // 8, 8, heads_width), axis=0)

        total = lax.fori_loop(0, width // deep, squares, jnp.zeros((8, heads_width), F32))
        mean_sq = jnp.sum(total, axis=0, keepdims=True) / width
        bound = (1.0 + codes[j].astype(F32)) * jnp.sqrt(mean_sq + 1e-06)
        inverse = 1.0 / bound

        def clip(i, carry, j=j, bound=bound, inverse=inverse):
            at = pl.ds(pl.multiple_of(i * deep, deep), deep)
            weights[j, at, :] = (bound * jnp.tanh(w[j, at, :].astype(F32) * inverse)).astype(BF16)
            return carry

        lax.fori_loop(0, width // deep, clip, 0)

    def norm(p, carry):
        at = pl.ds(pl.multiple_of(p * 32, 32), 32)
        xhat, _ = standardize(tok[at, :])
        normed[at, :] = (xhat * gain[...]).astype(BF16)
        return carry

    lax.fori_loop(0, rows // 32, norm, 0)
    low[...] = nn(normed[...], down[...]).astype(BF16)
    q[...] = (nn(normed[...], weights[0]) + nn(low[:, 0:rank], up[0])).astype(BF16)
    k[...] = nn(normed[...], weights[1]).astype(BF16)
    v[...] = (nn(normed[...], weights[2]) + nn(low[:, rank:], up[1])).astype(BF16)
    d_att[...] = nn(cot[...], w[3]).astype(BF16)

    pair = 2 * frames
    scale = HEAD_DIM ** (-0.5)
    t_at = lax.broadcasted_iota(jnp.int32, (pair, pair), 0)
    s_at = lax.broadcasted_iota(jnp.int32, (pair, pair), 1)
    allowed = (s_at <= t_at + offsets[0]) & (s_at // frames == t_at // frames)

    def attend(p, carry):
        at = pl.ds(pl.multiple_of(p * pair, pair), pair)
        for h in range(heads_width // HEAD_DIM):
            cols = slice(h * HEAD_DIM, (h + 1) * HEAD_DIM)
            qh, kh, vh, doh = q[at, cols], k[at, cols], v[at, cols], d_att[at, cols]
            masked = jnp.where(allowed, nt(qh, kh) * scale, -1e30)
            expo = jnp.exp(masked - jnp.max(masked, axis=1, keepdims=True))
            prob = expo / jnp.sum(expo, axis=1, keepdims=True)
            prob_b = prob.astype(BF16)
            ah = nn(prob_b, vh).astype(BF16)
            att[at, cols] = ah
            delta = jnp.sum(doh.astype(F32) * ah.astype(F32), axis=1, keepdims=True)
            d_score = (prob * (nt(doh, vh) - delta)).astype(BF16)
            grads[0, at, cols] = (nn(d_score, kh) * scale).astype(BF16)
            grads[1, at, cols] = (tn(d_score, qh) * scale).astype(BF16)
            grads[2, at, cols] = tn(prob_b, doh).astype(BF16)
        return carry

    lax.fori_loop(0, n_patch // 2, attend, 0)
    d_low = jnp.concatenate((nt(grads[0], up[0]), nt(grads[2], up[1])), axis=1).astype(BF16)
    up_part[0] = tn(low[:, 0:rank], grads[0])
    up_part[1] = tn(low[:, rank:], grads[2])

    def outward(n, carry):
        at = pl.ds(pl.multiple_of(n * heads_width, heads_width), heads_width)
        mixture[:, at] = nt(att[...], w[3, at, :]).astype(BF16)
        d_normed[:, at] = (
            nt(grads[0], weights[0, at, :])
            + nt(grads[1], weights[1, at, :])
            + nt(grads[2], weights[2, at, :])
            + nt(d_low, down[at, :])
        ).astype(BF16)
        down_part[n] = tn(d_low, normed[:, at])
        return carry

    lax.fori_loop(0, width // heads_width, outward, 0)


def local_block(tok, cot, w, gain, down, up, codes, offsets, frames):
    rows, width = tok.shape
    heads_width, rank = up.shape[2], up.shape[1]
    act = pltpu.VMEM((rows, heads_width), BF16)
    flat = jax.ShapeDtypeStruct((rows, width), BF16)
    return pl.pallas_call(
        functools.partial(block_kernel, frames),
        out_shape=(
            flat,
            flat,
            jax.ShapeDtypeStruct((width // heads_width, 2 * rank, heads_width), F32),
            jax.ShapeDtypeStruct((2, rank, heads_width), F32),
        ),
        in_specs=[SMEM, SMEM] + [VMEM] * 6,
        out_specs=(VMEM,) * 4,
        scratch_shapes=[
            pltpu.VMEM((3, width, heads_width), BF16),
            pltpu.VMEM((rows, width), BF16),
            act, act, act, act, act,
            pltpu.VMEM((3, rows, heads_width), BF16),
            pltpu.VMEM((rows, 2 * rank), BF16),
        ],
        compiler_params=pltpu.CompilerParams(vmem_limit_bytes=48 << 20),
    )(codes, offsets, tok, cot, w, gain.reshape(1, width), down.transpose(1, 0, 2).reshape(width, 2 * rank), up)


def return_kernel(
    n_dp, n_tm, n_tensor, mix, d_normed, all_tok, all_cot, gain, down_part, up_part,
    out_back, grad_back, total, down_all,
    own_rows, mine, near_in, far_out, far_in, staged, down_in, part, first, second, sums,
    fetch, near_send, near_recv, far_send, far_recv, down_send, down_recv,
    swap_send, swap_recv, g_send, g_recv,
):
    x, tm, t = lax.axis_index("dp"), lax.axis_index("tm"), lax.axis_index("tensor")
    z, yh = tm % Z, tm // Z
    n_half = n_tm // Z
    n_group = n_dp * n_half
    r = x * n_half + yh
    near = t + 1 - 2 * (t % 2)
    far = (t + 2) % n_tensor
    near_far = (near + 2) % n_tensor
    parts = (mix, d_normed)
    own_copies = [
        pltpu.make_async_copy(src.at[t], own_rows.at[k], fetch.at[k]) for k, src in enumerate((all_tok, all_cot))
    ]
    for k in range(2):
        own_copies.append(pltpu.make_async_copy(parts[k].at[t], mine.at[k, 0], fetch.at[2 + k]))
        own_copies.append(pltpu.make_async_copy(parts[k].at[far], mine.at[k, 1], fetch.at[4 + k]))
    for copy in own_copies:
        copy.start()
    greet(
        (
            (lambda d: {"tm": (tm + d) % n_tm}, n_tm - 1),
            (lambda d: {"tensor": (t + d) % n_tensor}, n_tensor - 1),
            (lambda d: {"dp": (x + d) % n_dp}, n_dp - 1),
            (lambda d: {"dp": (x + d) % n_dp, "tm": (tm + Z) % n_tm}, n_dp - 1),
        )
    )
    for k in range(2):
        remote(parts[k].at[near_far], near_in.at[k, 1], near_send, near_recv.at[k, 1], tensor=near).start()
        remote(parts[k].at[near], near_in.at[k, 0], near_send, near_recv.at[k, 0], tensor=near).start()
    down_in[t] = down_part[t]
    for d in range(1, n_tensor):
        peer = (t + d) % n_tensor
        remote(down_part.at[peer], down_in.at[t], down_send, down_recv, tensor=peer).start()
    for copy in own_copies:
        copy.wait()
    steps = own_rows.shape[1] // CHUNK
    for k in range(2):
        await_bytes(near_in.at[k, 1], near_recv.at[k, 1])

        def add_far(i, carry, k=k):
            at = pl.ds(pl.multiple_of(i * CHUNK, CHUNK), CHUNK)
            far_out[k, at, :] = (mine[k, 1, at, :].astype(F32) + near_in[k, 1, at, :].astype(F32)).astype(BF16)
            return carry

        lax.fori_loop(0, steps, add_far, 0)
        remote(far_out.at[k], far_in.at[k], far_send.at[k], far_recv.at[k], tensor=far).start()

    def to_group(pick, dst, stage):
        def one(d, carry):
            peer = (r + d) % n_group
            remote(
                pick(peer), dst.at[r], g_send.at[stage], g_recv.at[stage],
                dp=peer // n_half, tm=(peer % n_half) * Z + z,
            ).start()
            return carry

        lax.fori_loop(1, n_group, one, 0)

    await_bytes(down_in.at[pl.ds(0, n_tensor - 1)], down_recv)
    for a in range(n_group // 2):
        n_rows = part.shape[1]
        part[a] = jnp.sum(down_in[:, a * n_rows : (a + 1) * n_rows, :], axis=0)
        part[n_group // 2 + a] = up_part[a * n_rows : (a + 1) * n_rows, :]
    to_group(lambda peer: part.at[peer], first, 0)
    first[r] = part[r]

    def total_of(k, at):
        return mine[k, 0, at, :].astype(F32) + near_in[k, 0, at, :].astype(F32) + far_in[k, at, :].astype(F32)

    def stage(k, i, rows):
        staged[k, pl.ds(i * (CHUNK // 2), CHUNK // 2)] = rows.reshape(CHUNK // 2, 2, -1).astype(BF16)

    def send(k, dst):
        pltpu.make_async_copy(staged.at[k, tm], dst.at[tm], swap_recv.at[k]).start()

        def send_one(d, carry):
            peer = (tm + d) % n_tm
            remote(staged.at[k, peer], dst.at[tm], swap_send.at[k], swap_recv.at[k], tm=peer).start()
            return carry

        lax.fori_loop(1, n_tm, send_one, 0)

    await_bytes(near_in.at[0, 0], near_recv.at[0, 0])
    await_bytes(far_in.at[0], far_recv.at[0])

    def finish_out(i, carry):
        at = pl.ds(pl.multiple_of(i * CHUNK, CHUNK), CHUNK)
        stage(0, i, own_rows[0, at, :].astype(F32) + total_of(0, at))
        return carry

    lax.fori_loop(0, steps, finish_out, 0)
    send(0, out_back)
    await_bytes(near_in.at[1, 0], near_recv.at[1, 0])
    await_bytes(far_in.at[1], far_recv.at[1])

    def finish_grad(i, carry):
        at = pl.ds(pl.multiple_of(i * CHUNK, CHUNK), CHUNK)
        xhat, rstd = standardize(own_rows[0, at, :])
        g = total_of(1, at) * gain[...]
        m1 = jnp.mean(g, axis=-1, keepdims=True)
        m2 = jnp.mean(g * xhat, axis=-1, keepdims=True)
        stage(1, i, own_rows[1, at, :].astype(F32) + rstd * (g - m1 - xhat * m2))
        return carry

    lax.fori_loop(0, steps, finish_grad, 0)
    send(1, grad_back)

    await_bytes(first.at[pl.ds(0, n_group - 1)], g_recv.at[0])
    sums[0] = jnp.sum(first[...], axis=0)
    second[z] = sums[0]

    def along_z(d, carry):
        peer = (z + d) % Z
        remote(sums.at[0], second.at[z], g_send.at[1], g_recv.at[1], tm=yh * Z + peer).start()
        return carry

    lax.fori_loop(1, Z, along_z, 0)
    await_bytes(second.at[pl.ds(0, Z - 1)], g_recv.at[1])
    sums[1] = jnp.sum(second[...], axis=0)
    total[r] = sums[1]
    to_group(lambda peer: sums.at[1], total, 2)
    await_bytes(total.at[pl.ds(0, n_group - 1)], g_recv.at[2])
    half = pl.ds(0, n_group // 2)
    for d in range(1, n_tensor):
        remote(
            total.at[half], down_all.at[t], g_send.at[3], g_recv.at[3], tensor=(t + d) % n_tensor
        ).start()
    down_all[t] = total[half]
    await_bytes(down_all.at[pl.ds(0, n_tensor - 1)], g_recv.at[3])
    await_bytes(first.at[pl.ds(0, n_group - 1)], g_send.at[0])
    await_bytes(second.at[pl.ds(0, Z - 1)], g_send.at[1])
    await_bytes(first.at[pl.ds(0, n_group - 1)], g_send.at[2])
    await_bytes(down_all.at[pl.ds(0, n_tensor - 1)], g_send.at[3])
    await_bytes(near_in, near_send)
    await_bytes(down_in.at[pl.ds(0, n_tensor - 1)], down_send)
    for k, dst in ((0, out_back), (1, grad_back)):
        await_bytes(far_in.at[k], far_send.at[k])
        await_bytes(dst, swap_recv.at[k])
        await_bytes(staged.at[k, pl.ds(0, n_tm - 1)], swap_send.at[k])


def send_back(mix, d_normed, all_tok, all_cot, gain, down_part, up_part, shape, sizes):
    n_dp, n_tm, n_tensor = sizes
    n_group = n_dp * n_tm // Z
    rows, width = all_tok.shape[1:]
    tall, heads_width = up_part.shape
    chunk = (2 * tall // n_group, heads_width)
    flat = pltpu.VMEM((2, rows, width), BF16)
    same = jax.ShapeDtypeStruct(shape, BF16)
    return pl.pallas_call(
        functools.partial(return_kernel, n_dp, n_tm, n_tensor),
        out_shape=(
            same,
            same,
            jax.ShapeDtypeStruct((n_group,) + chunk, F32),
            jax.ShapeDtypeStruct((n_tensor, n_group // 2) + chunk, F32),
        ),
        in_specs=[ANY] * 4 + [VMEM] * 3,
        out_specs=(ANY, ANY, VMEM, VMEM),
        scratch_shapes=[
            flat,
            pltpu.VMEM((2, 2, rows, width), BF16),
            pltpu.VMEM((2, 2, rows, width), BF16),
            flat,
            flat,
            pltpu.VMEM((2,) + shape, BF16),
            pltpu.VMEM(down_part.shape, F32),
            pltpu.VMEM((n_group,) + chunk, F32),
            pltpu.VMEM((n_group,) + chunk, F32),
            pltpu.VMEM((Z,) + chunk, F32),
            pltpu.VMEM((2,) + chunk, F32),
            DMA((6,)), DMA, DMA((2, 2)), DMA((2,)), DMA((2,)), DMA, DMA,
            DMA((2,)), DMA((2,)), DMA((4,)), DMA((4,)),
        ],
        compiler_params=pltpu.CompilerParams(
            collective_id=1, has_side_effects=True, vmem_limit_bytes=32 << 20
        ),
    )(mix, d_normed, all_tok, all_cot, gain.reshape(1, width), down_part, up_part)


def on_device(tokens, gain, qkv, out, down, up, codes, offsets, cotangent):
    sizes = tuple(lax.axis_size(a) for a in ("dp", "tm", "tensor"))
    n_dp, n_tm, n_tensor = sizes
    width = tokens.shape[-1]
    rank, heads_width = down.shape[2], qkv.shape[2]
    all_tok, all_cot, w = gather(tokens[0], cotangent[0], qkv, out.T, codes, sizes)
    rows = all_tok.shape[1]
    mixture, d_normed, down_part, up_part = local_block(
        all_tok.reshape(-1, width),
        all_cot.reshape(-1, width),
        w.reshape(4, width, heads_width),
        gain, down, up, codes, offsets, rows,
    )
    block_out, grad_tokens, total, down_all = send_back(
        mixture.reshape(n_tensor, rows, width),
        d_normed.reshape(n_tensor, rows, width),
        all_tok, all_cot, gain, down_part, up_part.reshape(2 * rank, heads_width),
        tokens.shape[1:], sizes,
    )
    grad_up = total.reshape(2, 2, rank, heads_width)[1]
    grad_down = down_all.reshape(n_tensor, 2, rank, heads_width).transpose(1, 0, 3, 2)
    return block_out[None], grad_tokens[None], grad_down.reshape(2, width, rank), grad_up


def solution(mesh):
    return jax.shard_map(
        on_device,
        mesh=mesh,
        in_specs=(
            P("dp", "tensor", "tm", None),
            P(),
            P(None, "tm", "tensor"),
            P("tensor", "tm"),
            P(),
            P(None, None, "tensor"),
            P(),
            P("dp"),
            P("dp", "tensor", "tm", None),
        ),
        out_specs=(
            P("dp", "tensor", "tm", None),
            P("dp", "tensor", "tm", None),
            P(),
            P(None, None, "tensor"),
        ),
        check_vma=False,
    )
```

```python
import functools

import jax
import jax.numpy as jnp
from jax import lax
from jax.experimental import pallas as pl
from jax.experimental.pallas import tpu as pltpu
from jax.sharding import PartitionSpec as P

MESH = pl.DeviceIdType.MESH
ANY = pl.BlockSpec(memory_space=pl.ANY)
VMEM = pl.BlockSpec(memory_space=pltpu.VMEM)
SMEM = pl.BlockSpec(memory_space=pltpu.SMEM)
DMA = pltpu.SemaphoreType.DMA
Z = 16
CHUNK = 16

HEAD_DIM = 128
F32 = jnp.float32
BF16 = jnp.bfloat16


def standardize(rows):
    wide = rows.astype(F32)
    removed = wide - jnp.mean(wide, axis=-1, keepdims=True)
    rstd = lax.rsqrt(jnp.mean(removed * removed, axis=-1, keepdims=True) + 1e-05)
    return removed * rstd, rstd


def remote(src, dst, send, recv, **where):
    return pltpu.make_async_remote_copy(
        src_ref=src, dst_ref=dst, send_sem=send, recv_sem=recv, device_id=where, device_id_type=MESH
    )


def await_bytes(ref, sem):
    pltpu.make_async_copy(ref, ref, sem).wait()


def nn(a, b):
    return jnp.dot(a, b, preferred_element_type=F32)


def nt(a, b):
    return lax.dot_general(a, b, (((1,), (1,)), ((), ())), preferred_element_type=F32)


def tn(a, b):
    return lax.dot_general(a, b, (((0,), (0,)), ((), ())), preferred_element_type=F32)


def fused_kernel(
    n_dp, n_tm, n_tensor, frames, codes, offsets, tok, cot, qkv, out_t, gain, down, up,
    out_back, grad_back, total, down_all,
    shard, sq, landed, rows_all, w, weights, normed, q, k, v, att, d_att, grads, low, probs,
    parts, near_in, far_out, far_in, staged, down_part, up_part, down_in, part, first, second, wide_sum, sent_sum,
    sq_send, sq_recv, swap_send, swap_recv, spread_send, spread_far, spread_near,
    z_send, z_recv, y_send, y_first, y_recv, x_send, x_recv, local,
    near_send, near_recv, far_send, far_recv, down_send, down_recv, back_send, back_recv, g_send, g_recv,
):
    x, tm, t = lax.axis_index("dp"), lax.axis_index("tm"), lax.axis_index("tensor")
    z, yh = tm % Z, tm // Z
    up_z = yh * Z + (z + 1) % Z
    down_z = yh * Z + (z + Z - 1) % Z
    other = (tm + Z) % n_tm
    near = t + 1 - 2 * (t % 2)
    far = (t + 2) % n_tensor
    near_far = (near + 2) % n_tensor
    mats = (x, (x + 2) % n_dp)
    n_half = n_tm // Z
    n_group = n_dp * n_half
    r = x * n_half + yh
    depth = qkv.shape[1]
    rows, width = normed.shape
    heads_width = q.shape[1]
    rank = up.shape[1]

    def block_of(tensor):
        return pl.ds(pl.multiple_of(tensor * frames, frames), frames)

    def piece_of(half, zs):
        return pl.ds(pl.multiple_of((half * Z + zs) * depth, depth), depth)

    def half_of(half):
        return pl.ds(pl.multiple_of(half * Z * depth, Z * depth), Z * depth)

    barrier = pltpu.get_barrier_semaphore()
    greeted = 0
    for count, address in (
        (n_tm - 1, lambda d: {"tm": (tm + d) % n_tm}),
        (n_tensor - 1, lambda d: {"tensor": (t + d) % n_tensor}),
        (n_dp - 1, lambda d: {"dp": (x + d) % n_dp}),
        (n_dp - 1, lambda d: {"dp": (x + d) % n_dp, "tm": other}),
    ):

        def greet(d, carry, address=address):
            pl.semaphore_signal(barrier, inc=1, device_id=address(d), device_id_type=MESH)
            return carry

        lax.fori_loop(1, count + 1, greet, 0)
        greeted += count
    wide = out_t[...].astype(F32)
    sq[t] = jnp.broadcast_to(jnp.sum(wide * wide, axis=1, keepdims=True), sq.shape[1:])
    for j in range(3):
        shard[j] = qkv[j]
    pl.semaphore_wait(barrier, greeted)

    for d in range(1, n_tensor):
        remote(sq.at[t], sq.at[t], sq_send, sq_recv, tensor=(t + d) % n_tensor).start()

    def swap(k_, src):
        pltpu.make_async_copy(src.at[tm], landed.at[k_, tm], swap_recv.at[k_]).start()

        def send_one(d, carry):
            peer = (tm + d) % n_tm
            remote(
                src.at[peer], landed.at[k_, tm], swap_send.at[k_], swap_recv.at[k_], tm=peer
            ).start()
            return carry

        lax.fori_loop(1, n_tm, send_one, 0)

    swap(0, tok)
    await_bytes(sq.at[pl.ds(0, n_tensor - 1)], sq_recv)
    mean_out = jnp.sum(sq[...], axis=0)[:, 0:1] / (n_tensor * out_t.shape[1])
    bound_out = (1.0 + codes[3].astype(F32)) * jnp.sqrt(mean_out + 1e-06)
    shard[3] = (bound_out * jnp.tanh(wide / bound_out)).astype(BF16)

    def to_z(src, i, piece, half, zs, step, up_side):
        side = 0 if up_side else 1
        remote(
            src, w.at[mats[i], piece_of(half, zs)], z_send.at[side], z_recv.at[side, step, piece],
            tm=up_z if up_side else down_z,
        ).start()

    def to_x(src, half, zs):
        for side, dest in ((0, (x + 1) % n_dp), (1, (x + n_dp - 1) % n_dp)):
            remote(src, w.at[x, piece_of(half, zs)], x_send.at[side], x_recv.at[side], dp=dest).start()

    def to_y(src, zs):
        remote(src, w.at[mats[1], piece_of(yh, zs)], y_send, y_recv, tm=other).start()

    remote(shard.at[x], w.at[x, piece_of(yh, z)], y_send, y_first, tm=other).start()
    for i in range(2):
        to_z(shard.at[mats[i]], i, i, yh, z, 0, True)
        to_z(shard.at[mats[i]], i, i, yh, z, 0, False)
    to_x(shard.at[x], yh, z)
    to_y(shard.at[mats[1]], z)
    for i in range(2):
        pltpu.make_async_copy(shard.at[mats[i]], w.at[mats[i], piece_of(yh, z)], local).start()
    swap(1, cot)
    here = w.at[x, piece_of(1 - yh, z)]
    await_bytes(here, y_first)
    to_z(here, 0, 2, 1 - yh, z, 0, True)
    to_z(here, 0, 2, 1 - yh, z, 0, False)
    to_x(here, 1 - yh, z)

    def arrive(step, up_side, onward):
        zs = (z + Z - 1 - step) % Z if up_side else (z + 1 + step) % Z
        side = 0 if up_side else 1
        for piece, (i, half) in enumerate(((0, yh), (1, yh), (0, 1 - yh))):
            here = w.at[mats[i], piece_of(half, zs)]
            await_bytes(here, z_recv.at[side, step, piece])
            if onward:
                to_z(here, i, piece, half, zs, step + 1, up_side)
            if i == 0:
                to_x(here, half, zs)
            else:
                to_y(here, zs)

    def ring(step, carry):
        arrive(step, True, True)
        arrive(step, False, True)
        return carry

    def spread(k_):
        await_bytes(landed.at[k_], swap_recv.at[k_])
        for i in range(frames // CHUNK):
            pairs = landed[k_, i * CHUNK // 2 : (i + 1) * CHUNK // 2].astype(F32)
            at = pl.ds(pl.multiple_of(t * frames + i * CHUNK, CHUNK), CHUNK)
            rows_all[k_, at, :] = pairs.reshape(CHUNK, -1).astype(BF16)
        mine = rows_all.at[k_, block_of(t)]
        remote(mine, mine, spread_send.at[k_], spread_far.at[k_], tensor=far).start()
        remote(mine, mine, spread_send.at[k_], spread_near.at[k_], tensor=near).start()

    def forward(k_):
        mine = rows_all.at[k_, block_of(far)]
        await_bytes(mine, spread_far.at[k_])
        remote(mine, mine, spread_send.at[k_], spread_near.at[k_], tensor=near).start()

    lax.fori_loop(0, 4, ring, 0)
    spread(0)
    lax.fori_loop(4, 6, ring, 0)
    spread(1)
    lax.fori_loop(6, Z // 2 - 2, ring, 0)
    arrive(Z // 2 - 2, True, True)
    arrive(Z // 2 - 2, False, False)
    arrive(Z // 2 - 1, True, False)
    forward(0)
    await_bytes(rows_all.at[0, pl.ds(0, 2 * frames)], spread_near.at[0])

    def norm(p, carry):
        at = pl.ds(pl.multiple_of(p * 32, 32), 32)
        xhat, _ = standardize(rows_all[0, at, :])
        normed[at, :] = (xhat * gain[...]).astype(BF16)
        return carry

    lax.fori_loop(0, rows // 32, norm, 0)
    for i in range(2):
        low[:, i * rank : (i + 1) * rank] = nn(normed[...], down[i]).astype(BF16)
    forward(1)

    deep = 192

    def clip_matrix(m):
        def squares(i, total_):
            block = w[m, pl.ds(pl.multiple_of(i * deep, deep), deep), :].astype(F32)
            return total_ + jnp.sum((block * block).reshape(deep // 8, 8, heads_width), axis=0)

        total_ = lax.fori_loop(0, width // deep, squares, jnp.zeros((8, heads_width), F32))
        mean_sq = jnp.sum(total_, axis=0, keepdims=True) / width
        bound = (1.0 + codes[m].astype(F32)) * jnp.sqrt(mean_sq + 1e-06)
        inverse = 1.0 / bound

        def clip(i, carry):
            at = pl.ds(pl.multiple_of(i * deep, deep), deep)
            weights[m, at, :] = (bound * jnp.tanh(w[m, at, :].astype(F32) * inverse)).astype(BF16)
            return carry

        lax.fori_loop(0, width // deep, clip, 0)

    await_bytes(shard.at[pl.ds(0, 2)], local)
    await_bytes(w.at[mats[1], half_of(1 - yh)], y_recv)
    order = (mats[0], mats[1], (x + n_dp - 1) % n_dp, (x + 1) % n_dp)
    for i, m in enumerate(order):
        if i >= 2:
            await_bytes(w.at[m], x_recv.at[i - 2])
        pl.when(m != 3)(functools.partial(clip_matrix, m))

    q[...] = (nn(normed[...], weights[0]) + nn(low[:, 0:rank], up[0])).astype(BF16)
    k[...] = nn(normed[...], weights[1]).astype(BF16)
    v[...] = (nn(normed[...], weights[2]) + nn(low[:, rank:], up[1])).astype(BF16)

    pair = 2 * frames
    heads = heads_width // HEAD_DIM
    scale = HEAD_DIM ** (-0.5)
    t_at = lax.broadcasted_iota(jnp.int32, (pair, pair), 0)
    s_at = lax.broadcasted_iota(jnp.int32, (pair, pair), 1)
    allowed = (s_at <= t_at + offsets[0]) & (s_at // frames == t_at // frames)

    def attend(p, carry):
        at = pl.ds(pl.multiple_of(p * pair, pair), pair)
        for h in range(heads):
            cols = slice(h * HEAD_DIM, (h + 1) * HEAD_DIM)
            masked = jnp.where(allowed, nt(q[at, cols], k[at, cols]) * scale, -1e30)
            expo = jnp.exp(masked - jnp.max(masked, axis=1, keepdims=True))
            prob = expo / jnp.sum(expo, axis=1, keepdims=True)
            probs[p * heads + h] = prob
            att[at, cols] = nn(prob.astype(BF16), v[at, cols]).astype(BF16)
        return carry

    lax.fori_loop(0, rows // pair, attend, 0)

    def mix(n, carry):
        at = pl.ds(pl.multiple_of(n * heads_width, heads_width), heads_width)
        parts[0, :, at] = nt(att[...], w[3, at, :]).astype(BF16)
        return carry

    lax.fori_loop(0, width // heads_width, mix, 0)

    def to_near(k_):
        for i, tensor in ((1, near_far), (0, near)):
            remote(
                parts.at[k_, block_of(tensor)], near_in.at[k_, i], near_send, near_recv.at[k_, i], tensor=near
            ).start()

    def to_far(k_):
        await_bytes(near_in.at[k_, 1], near_recv.at[k_, 1])

        def add(i, carry):
            at = pl.ds(pl.multiple_of(i * CHUNK, CHUNK), CHUNK)
            from_mine = pl.ds(pl.multiple_of(far * frames + i * CHUNK, CHUNK), CHUNK)
            far_out[k_, at, :] = (
                parts[k_, from_mine, :].astype(F32) + near_in[k_, 1, at, :].astype(F32)
            ).astype(BF16)
            return carry

        lax.fori_loop(0, frames // CHUNK, add, 0)
        remote(far_out.at[k_], far_in.at[k_], far_send.at[k_], far_recv.at[k_], tensor=far).start()

    def own_at(i):
        return pl.ds(pl.multiple_of(t * frames + i * CHUNK, CHUNK), CHUNK)

    def total_of(k_, i):
        at = pl.ds(pl.multiple_of(i * CHUNK, CHUNK), CHUNK)
        return (
            parts[k_, own_at(i), :].astype(F32)
            + near_in[k_, 0, at, :].astype(F32)
            + far_in[k_, at, :].astype(F32)
        )

    def stage(k_, i, value):
        staged[k_, pl.ds(i * (CHUNK // 2), CHUNK // 2)] = value.reshape(CHUNK // 2, 2, -1).astype(BF16)

    def send_back(k_, dst):
        pltpu.make_async_copy(staged.at[k_, tm], dst.at[tm], back_recv.at[k_]).start()

        def send_one(d, carry):
            peer = (tm + d) % n_tm
            remote(staged.at[k_, peer], dst.at[tm], back_send.at[k_], back_recv.at[k_], tm=peer).start()
            return carry

        lax.fori_loop(1, n_tm, send_one, 0)

    def await_parts(k_):
        await_bytes(near_in.at[k_, 0], near_recv.at[k_, 0])
        await_bytes(far_in.at[k_], far_recv.at[k_])

    to_near(0)
    await_bytes(rows_all.at[1, pl.ds(0, 2 * frames)], spread_near.at[1])
    d_att[...] = nn(rows_all[1], w[3]).astype(BF16)
    to_far(0)

    def attend_back(p, carry):
        at = pl.ds(pl.multiple_of(p * pair, pair), pair)
        for h in range(heads):
            cols = slice(h * HEAD_DIM, (h + 1) * HEAD_DIM)
            qh, kh, vh, doh = q[at, cols], k[at, cols], v[at, cols], d_att[at, cols]
            prob = probs[p * heads + h]
            delta = jnp.sum(doh.astype(F32) * att[at, cols].astype(F32), axis=1, keepdims=True)
            d_score = (prob * (nt(doh, vh) - delta)).astype(BF16)
            grads[0, at, cols] = (nn(d_score, kh) * scale).astype(BF16)
            grads[1, at, cols] = (tn(d_score, qh) * scale).astype(BF16)
            grads[2, at, cols] = tn(prob.astype(BF16), doh).astype(BF16)
        return carry

    lax.fori_loop(0, rows // pair, attend_back, 0)
    d_low = jnp.concatenate((nt(grads[0], up[0]), nt(grads[2], up[1])), axis=1).astype(BF16)
    up_part[0:rank] = tn(low[:, 0:rank], grads[0])
    up_part[rank:] = tn(low[:, rank:], grads[2])

    def outward(n, carry):
        at = pl.ds(pl.multiple_of(n * heads_width, heads_width), heads_width)
        down_part[n] = tn(d_low, normed[:, at])
        parts[1, :, at] = (
            nt(grads[0], weights[0, at, :])
            + nt(grads[1], weights[1, at, :])
            + nt(grads[2], weights[2, at, :])
            + nt(d_low[:, 0:rank], down[0, at, :])
            + nt(d_low[:, rank:], down[1, at, :])
        ).astype(BF16)
        return carry

    lax.fori_loop(0, width // heads_width, outward, 0)
    to_near(1)
    down_in[t] = down_part[t]
    for d in range(1, n_tensor):
        peer = (t + d) % n_tensor
        remote(down_part.at[peer], down_in.at[t], down_send, down_recv, tensor=peer).start()
    await_parts(0)

    def finish_out(i, carry):
        stage(0, i, rows_all[0, own_at(i), :].astype(F32) + total_of(0, i))
        return carry

    lax.fori_loop(0, frames // CHUNK, finish_out, 0)
    send_back(0, out_back)
    to_far(1)

    def to_group(pick, dst, stage_):
        def one(d, carry):
            peer = (r + d) % n_group
            remote(
                pick(peer), dst.at[r], g_send.at[stage_], g_recv.at[stage_],
                dp=peer // n_half, tm=(peer % n_half) * Z + z,
            ).start()
            return carry

        lax.fori_loop(1, n_group, one, 0)

    await_bytes(down_in.at[pl.ds(0, n_tensor - 1)], down_recv)
    n_rows = part.shape[1]
    for a in range(n_group // 2):
        part[a] = jnp.sum(down_in[:, a * n_rows : (a + 1) * n_rows, :], axis=0)
        part[n_group // 2 + a] = up_part[a * n_rows : (a + 1) * n_rows, :]
    to_group(lambda peer: part.at[peer], first, 0)
    first[r] = part[r]
    await_bytes(first.at[pl.ds(0, n_group - 1)], g_recv.at[0])
    sent_sum[0] = jnp.sum(first[...], axis=0).astype(BF16)
    second[z] = sent_sum[0]

    def along_z(d, carry):
        peer = (z + d) % Z
        remote(sent_sum.at[0], second.at[z], g_send.at[1], g_recv.at[1], tm=yh * Z + peer).start()
        return carry

    lax.fori_loop(1, Z, along_z, 0)
    await_parts(1)

    def finish_grad(i, carry):
        xhat, rstd = standardize(rows_all[0, own_at(i), :])
        g = total_of(1, i) * gain[...]
        m1 = jnp.mean(g, axis=-1, keepdims=True)
        m2 = jnp.mean(g * xhat, axis=-1, keepdims=True)
        stage(1, i, rows_all[1, own_at(i), :].astype(F32) + rstd * (g - m1 - xhat * m2))
        return carry

    lax.fori_loop(0, frames // CHUNK, finish_grad, 0)
    send_back(1, grad_back)
    await_bytes(second.at[pl.ds(0, Z - 1)], g_recv.at[1])
    wide_sum[0] = jnp.sum(second[...].astype(F32), axis=0)
    total[r] = wide_sum[0]
    to_group(lambda peer: wide_sum.at[0], total, 2)
    await_bytes(total.at[pl.ds(0, n_group - 1)], g_recv.at[2])
    lower = pl.ds(0, n_group // 2)
    for d in range(1, n_tensor):
        remote(
            total.at[lower], down_all.at[t], g_send.at[3], g_recv.at[3], tensor=(t + d) % n_tensor
        ).start()
    down_all[t] = total[lower]
    await_bytes(down_all.at[pl.ds(0, n_tensor - 1)], g_recv.at[3])

    await_bytes(sq.at[pl.ds(0, n_tensor - 1)], sq_send)
    for k_ in range(2):
        await_bytes(landed.at[k_, pl.ds(0, n_tm - 1)], swap_send.at[k_])
        await_bytes(rows_all.at[k_, pl.ds(0, 3 * frames)], spread_send.at[k_])
        await_bytes(far_in.at[k_], far_send.at[k_])
        await_bytes(w.at[0], x_send.at[k_])
    await_bytes(w.at[0, pl.ds(0, (Z + 1) * depth)], y_send)
    for j in range(3):
        await_bytes(w.at[0, pl.ds(0, Z // 2 * depth)], z_send.at[0])
        await_bytes(w.at[0, pl.ds(0, (Z // 2 - 1) * depth)], z_send.at[1])
    await_bytes(near_in, near_send)
    await_bytes(down_in.at[pl.ds(0, n_tensor - 1)], down_send)
    await_bytes(first.at[pl.ds(0, n_group - 1)], g_send.at[0])
    await_bytes(second.at[pl.ds(0, Z - 1)], g_send.at[1])
    await_bytes(first.at[pl.ds(0, n_group - 1)], g_send.at[2])
    await_bytes(down_all.at[pl.ds(0, n_tensor - 1)], g_send.at[3])
    for k_, dst in ((0, out_back), (1, grad_back)):
        await_bytes(dst, back_recv.at[k_])
        await_bytes(staged.at[k_, pl.ds(0, n_tm - 1)], back_send.at[k_])


def fused(tok, cot, qkv, out_t, gain, down, up, codes, offsets, sizes):
    n_dp, n_tm, n_tensor = sizes
    patches, few, width = tok.shape
    frames = patches * few
    rows = n_tensor * frames
    rank, heads_width = up.shape[1:]
    n_group = n_dp * n_tm // Z
    chunk = (4 * rank // n_group, heads_width)
    pair = 2 * frames

    def bf16(*shape):
        return pltpu.VMEM(shape, BF16)

    def f32(*shape):
        return pltpu.VMEM(shape, F32)

    act = bf16(rows, heads_width)
    same = jax.ShapeDtypeStruct(tok.shape, BF16)
    return pl.pallas_call(
        functools.partial(fused_kernel, n_dp, n_tm, n_tensor, frames),
        out_shape=(
            same,
            same,
            jax.ShapeDtypeStruct((n_group,) + chunk, F32),
            jax.ShapeDtypeStruct((n_tensor, n_group // 2) + chunk, F32),
        ),
        in_specs=[SMEM, SMEM, ANY, ANY] + [VMEM] * 5,
        out_specs=(ANY, ANY, VMEM, VMEM),
        scratch_shapes=[
            bf16(4, qkv.shape[1], heads_width),
            f32(n_tensor, out_t.shape[0], 128),
            bf16(2, *tok.shape),
            bf16(2, rows, width),
            bf16(4, width, heads_width),
            bf16(3, width, heads_width),
            bf16(rows, width),
            act, act, act, act, act,
            bf16(3, rows, heads_width),
            bf16(rows, 2 * rank),
            f32(rows // pair * (heads_width // HEAD_DIM), pair, pair),
            bf16(2, rows, width),
            bf16(2, 2, frames, width),
            bf16(2, frames, width),
            bf16(2, frames, width),
            bf16(2, *tok.shape),
            f32(width // heads_width, 2 * rank, heads_width),
            f32(2 * rank, heads_width),
            f32(n_tensor, 2 * rank, heads_width),
            f32(n_group, *chunk),
            f32(n_group, *chunk),
            bf16(Z, *chunk),
            f32(1, *chunk),
            bf16(1, *chunk),
            DMA, DMA, DMA((2,)), DMA((2,)), DMA((2,)), DMA((2,)), DMA((2,)),
            DMA((2,)), DMA((2, Z // 2, 3)), DMA, DMA, DMA, DMA((2,)), DMA((2,)), DMA,
            DMA, DMA((2, 2)), DMA((2,)), DMA((2,)), DMA, DMA, DMA((2,)), DMA((2,)), DMA((4,)), DMA((4,)),
        ],
        compiler_params=pltpu.CompilerParams(
            collective_id=0, has_side_effects=True, vmem_limit_bytes=56 << 20
        ),
    )(codes, offsets, tok, cot, qkv, out_t, gain.reshape(1, width), down, up)


def on_device(tokens, gain, qkv, out, down, up, codes, offsets, cotangent):
    sizes = tuple(lax.axis_size(a) for a in ("dp", "tm", "tensor"))
    n_tensor = sizes[2]
    width = tokens.shape[-1]
    rank, heads_width = down.shape[2], qkv.shape[2]
    block_out, grad_tokens, total, down_all = fused(
        tokens[0], cotangent[0], qkv, out.T, gain, down, up, codes, offsets, sizes
    )
    grad_up = total.reshape(2, 2, rank, heads_width)[1]
    grad_down = down_all.reshape(n_tensor, 2, rank, heads_width).transpose(1, 0, 3, 2)
    return block_out[None], grad_tokens[None], grad_down.reshape(2, width, rank), grad_up


def solution(mesh):
    return jax.shard_map(
        on_device,
        mesh=mesh,
        in_specs=(
            P("dp", "tensor", "tm", None),
            P(),
            P(None, "tm", "tensor"),
            P("tensor", "tm"),
            P(),
            P(None, None, "tensor"),
            P(),
            P("dp"),
            P("dp", "tensor", "tm", None),
        ),
        out_specs=(
            P("dp", "tensor", "tm", None),
            P("dp", "tensor", "tm", None),
            P(),
            P(None, None, "tensor"),
        ),
        check_vma=False,
    )
```

```python
import functools

import jax
import jax.numpy as jnp
from jax import lax
from jax.experimental import pallas as pl
from jax.experimental.pallas import tpu as pltpu
from jax.sharding import PartitionSpec as P

MESH = pl.DeviceIdType.MESH
ANY = pl.BlockSpec(memory_space=pl.ANY)
VMEM = pl.BlockSpec(memory_space=pltpu.VMEM)
SMEM = pl.BlockSpec(memory_space=pltpu.SMEM)
DMA = pltpu.SemaphoreType.DMA
Z = 16
CHUNK = 16

HEAD_DIM = 128
F32 = jnp.float32
BF16 = jnp.bfloat16


def standardize(rows):
    wide = rows.astype(F32)
    removed = wide - jnp.mean(wide, axis=-1, keepdims=True)
    rstd = lax.rsqrt(jnp.mean(removed * removed, axis=-1, keepdims=True) + 1e-05)
    return removed * rstd, rstd


def remote(src, dst, send, recv, **where):
    return pltpu.make_async_remote_copy(
        src_ref=src, dst_ref=dst, send_sem=send, recv_sem=recv, device_id=where, device_id_type=MESH
    )


def await_bytes(ref, sem):
    pltpu.make_async_copy(ref, ref, sem).wait()


def nn(a, b):
    return jnp.dot(a, b, preferred_element_type=F32)


def nt(a, b):
    return lax.dot_general(a, b, (((1,), (1,)), ((), ())), preferred_element_type=F32)


def tn(a, b):
    return lax.dot_general(a, b, (((0,), (0,)), ((), ())), preferred_element_type=F32)


def fused_kernel(
    n_dp, n_tm, n_tensor, frames, codes, offsets, tok, cot, qkv, out_t, gain, down, up,
    out_back, grad_back, grad_down, grad_up,
    total, down_all, shard, sq, column, landed, rows_all, w, normed, q, k, v, att, d_att, grads, low, probs,
    parts, near_in, far_out, far_in, staged, down_part, up_part, down_in, part, first, fours, wide_sum, sent_sum,
    column_send, column_recv, sq_send, sq_recv, swap_send, swap_recv, spread_send, spread_far, spread_near,
    z_send, z_recv, y_send, y_first, y_recv, x_send, x_recv, local,
    near_send, near_first, near_recv, far_send, far_recv, down_send, down_recv, back_send, back_recv, g_send, g_recv, z_send_sum, z_recv_sum,
):
    x, tm, t = lax.axis_index("dp"), lax.axis_index("tm"), lax.axis_index("tensor")
    z, yh = tm % Z, tm // Z
    up_z = yh * Z + (z + 1) % Z
    down_z = yh * Z + (z + Z - 1) % Z
    other = (tm + Z) % n_tm
    near = t + 1 - 2 * (t % 2)
    far = (t + 2) % n_tensor
    near_far = (near + 2) % n_tensor
    mats = (x, (x + 2) % n_dp)
    n_half = n_tm // Z
    n_group = n_dp * n_half
    r = x * n_half + yh
    depth = qkv.shape[1]
    rows, width = normed.shape
    heads_width = q.shape[1]
    rank = up.shape[1]

    def block_of(tensor):
        return pl.ds(pl.multiple_of(tensor * frames, frames), frames)

    def piece_of(half, zs):
        return pl.ds(pl.multiple_of((half * Z + zs) * depth, depth), depth)

    def half_of(half):
        return pl.ds(pl.multiple_of(half * Z * depth, Z * depth), Z * depth)

    barrier = pltpu.get_barrier_semaphore()
    greeted = 0
    for count, address in (
        (n_tm - 1, lambda d: {"tm": (tm + d) % n_tm}),
        (n_tensor - 1, lambda d: {"tensor": (t + d) % n_tensor}),
        (n_dp - 1, lambda d: {"dp": (x + d) % n_dp}),
        (n_dp - 1, lambda d: {"dp": (x + d) % n_dp, "tm": other}),
    ):

        def greet(d, carry, address=address):
            pl.semaphore_signal(barrier, inc=1, device_id=address(d), device_id_type=MESH)
            return carry

        lax.fori_loop(1, count + 1, greet, 0)
        greeted += count
    wide = out_t[...].astype(F32)
    sq[t] = jnp.broadcast_to(jnp.sum(wide * wide, axis=1, keepdims=True), sq.shape[1:])
    for j in range(3):
        shard[j] = qkv[j]
    shard[3] = out_t[...]
    for i in range(2):
        block = shard[mats[i]].astype(F32)
        column[tm, i : i + 1, :] = jnp.sum(block * block, axis=0, keepdims=True)
    pl.semaphore_wait(barrier, greeted)

    def send_column(d, carry):
        peer = (tm + d) % n_tm
        remote(column.at[tm], column.at[tm], column_send, column_recv, tm=peer).start()
        return carry

    lax.fori_loop(1, n_tm, send_column, 0)
    for d in range(1, n_tensor):
        remote(sq.at[t], sq.at[t], sq_send, sq_recv, tensor=(t + d) % n_tensor).start()

    sources = (tok, cot)
    for k_ in range(2):
        pltpu.make_async_copy(sources[k_].at[tm], landed.at[k_, tm], swap_recv.at[k_]).start()

    def swap(first_, last):
        for k_ in range(2):

            def send_one(d, carry, k_=k_):
                peer = (tm + d) % n_tm
                remote(
                    sources[k_].at[peer], landed.at[k_, tm], swap_send.at[k_], swap_recv.at[k_], tm=peer
                ).start()
                return carry

            least = k_ * (n_tm - 1)
            low_, high_ = (jnp.clip(at - least, 0, n_tm - 1) for at in (first_, last))
            lax.fori_loop(1 + low_, 1 + high_, send_one, 0)

    swap(0, 31)
    await_bytes(sq.at[pl.ds(0, n_tensor - 1)], sq_recv)
    mean_out = jnp.sum(sq[...], axis=0)[:, 0:1] / (n_tensor * out_t.shape[1])
    bound_out = (1.0 + codes[3].astype(F32)) * jnp.sqrt(mean_out + 1e-06)
    await_bytes(column.at[pl.ds(0, n_tm - 1)], column_recv)
    mean_in = jnp.sum(column[...], axis=0) / width
    for i, m in enumerate(mats):

        def clip_columns(i=i, m=m):
            bound = (1.0 + codes[m].astype(F32)) * jnp.sqrt(mean_in[i : i + 1] + 1e-06)
            shard[m] = (bound * jnp.tanh(shard[m].astype(F32) / bound)).astype(BF16)

        def clip_rows():
            shard[3] = (bound_out * jnp.tanh(wide / bound_out)).astype(BF16)

        pl.when(m != 3)(clip_columns)
        pl.when(m == 3)(clip_rows)

    def to_z(src, i, piece, half, zs, step, up_side):
        side = 0 if up_side else 1
        remote(
            src, w.at[mats[i], piece_of(half, zs)], z_send.at[side], z_recv.at[side, step, piece],
            tm=up_z if up_side else down_z,
        ).start()

    def to_x(src, half, zs):
        for side, dest in ((0, (x + 1) % n_dp), (1, (x + n_dp - 1) % n_dp)):
            remote(src, w.at[x, piece_of(half, zs)], x_send.at[side], x_recv.at[side], dp=dest).start()

    def to_y(src, zs):
        remote(src, w.at[mats[1], piece_of(yh, zs)], y_send, y_recv, tm=other).start()

    remote(shard.at[x], w.at[x, piece_of(yh, z)], y_send, y_first, tm=other).start()
    for i in range(2):
        to_z(shard.at[mats[i]], i, i, yh, z, 0, True)
        to_z(shard.at[mats[i]], i, i, yh, z, 0, False)
    to_x(shard.at[x], yh, z)
    to_y(shard.at[mats[1]], z)
    for i in range(2):
        pltpu.make_async_copy(shard.at[mats[i]], w.at[mats[i], piece_of(yh, z)], local).start()
    here = w.at[x, piece_of(1 - yh, z)]
    await_bytes(here, y_first)
    to_z(here, 0, 2, 1 - yh, z, 0, True)
    to_z(here, 0, 2, 1 - yh, z, 0, False)
    to_x(here, 1 - yh, z)

    def arrive(step, up_side, onward):
        zs = (z + Z - 1 - step) % Z if up_side else (z + 1 + step) % Z
        side = 0 if up_side else 1
        for piece, (i, half) in enumerate(((0, yh), (1, yh), (0, 1 - yh))):
            here = w.at[mats[i], piece_of(half, zs)]
            await_bytes(here, z_recv.at[side, step, piece])
            if onward:
                to_z(here, i, piece, half, zs, step + 1, up_side)
            if i == 0:
                to_x(here, half, zs)
            else:
                to_y(here, zs)

    def ring(step, carry):
        arrive(step, True, True)
        arrive(step, False, True)
        swap(31 + step * 10, 31 + (step + 1) * 10)
        return carry

    def spread(k_):
        await_bytes(landed.at[k_], swap_recv.at[k_])
        for i in range(frames // CHUNK):
            pairs = landed[k_, i * CHUNK // 2 : (i + 1) * CHUNK // 2].astype(F32)
            at = pl.ds(pl.multiple_of(t * frames + i * CHUNK, CHUNK), CHUNK)
            rows_all[k_, at, :] = pairs.reshape(CHUNK, -1).astype(BF16)
        mine = rows_all.at[k_, block_of(t)]
        remote(mine, mine, spread_send.at[k_], spread_far.at[k_], tensor=far).start()
        remote(mine, mine, spread_send.at[k_], spread_near.at[k_], tensor=near).start()

    def forward(k_):
        mine = rows_all.at[k_, block_of(far)]
        await_bytes(mine, spread_far.at[k_])
        remote(mine, mine, spread_send.at[k_], spread_near.at[k_], tensor=near).start()

    lax.fori_loop(0, 5, ring, 0)
    spread(0)
    lax.fori_loop(5, Z // 2 - 2, ring, 0)
    swap(31 + (Z // 2 - 2) * 10, 2 * (n_tm - 1))
    arrive(Z // 2 - 2, True, True)
    arrive(Z // 2 - 2, False, False)
    arrive(Z // 2 - 1, True, False)
    spread(1)
    forward(0)
    await_bytes(rows_all.at[0, pl.ds(0, 2 * frames)], spread_near.at[0])

    def norm(p, carry):
        at = pl.ds(pl.multiple_of(p * 32, 32), 32)
        xhat, _ = standardize(rows_all[0, at, :])
        normed[at, :] = (xhat * gain[...]).astype(BF16)
        return carry

    lax.fori_loop(0, rows // 32, norm, 0)
    for i in range(2):
        low[:, i * rank : (i + 1) * rank] = nt(normed[...], down[i]).astype(BF16)

    await_bytes(shard.at[pl.ds(0, 2)], local)
    await_bytes(w.at[mats[1], half_of(1 - yh)], y_recv)
    await_bytes(w.at[(x + n_dp - 1) % n_dp], x_recv.at[0])
    await_bytes(w.at[(x + 1) % n_dp], x_recv.at[1])
    q[...] = (nn(normed[...], w[0]) + nn(low[:, 0:rank], up[0])).astype(BF16)
    k[...] = nn(normed[...], w[1]).astype(BF16)
    v[...] = (nn(normed[...], w[2]) + nn(low[:, rank:], up[1])).astype(BF16)

    pair = 2 * frames
    heads = heads_width // HEAD_DIM
    scale = HEAD_DIM ** (-0.5)
    t_at = lax.broadcasted_iota(jnp.int32, (pair, pair), 0)
    s_at = lax.broadcasted_iota(jnp.int32, (pair, pair), 1)
    allowed = (s_at <= t_at + offsets[0]) & (s_at // frames == t_at // frames)

    def attend(p, carry):
        at = pl.ds(pl.multiple_of(p * pair, pair), pair)
        for h in range(heads):
            cols = slice(h * HEAD_DIM, (h + 1) * HEAD_DIM)
            masked = jnp.where(allowed, nt(q[at, cols], k[at, cols]) * scale, -1e30)
            expo = jnp.exp(masked - jnp.max(masked, axis=1, keepdims=True))
            prob = expo / jnp.sum(expo, axis=1, keepdims=True)
            probs[p * heads + h] = prob
            att[at, cols] = nn(prob.astype(BF16), v[at, cols]).astype(BF16)
        return carry

    lax.fori_loop(0, rows // pair, attend, 0)

    def columns(n):
        return pl.ds(pl.multiple_of(n * heads_width, heads_width), heads_width)

    def to_near(k_, n):
        for i, tensor, sem in ((1, near_far, near_first.at[k_, n]), (0, near, near_recv.at[k_])):
            remote(
                parts.at[k_, block_of(tensor), columns(n)], near_in.at[k_, i, :, columns(n)], near_send, sem,
                tensor=near,
            ).start()

    def to_far(k_, n):
        at = columns(n)
        await_bytes(near_in.at[k_, 1, :, at], near_first.at[k_, n])
        far_out[k_, :, at] = (
            parts[k_, block_of(far), at].astype(F32) + near_in[k_, 1, :, at].astype(F32)
        ).astype(BF16)
        remote(
            far_out.at[k_, :, at], far_in.at[k_, :, at], far_send.at[k_], far_recv.at[k_], tensor=far
        ).start()

    def chunk_done(k_, n):
        to_near(k_, n)

        @pl.when(n > 0)
        def _():
            to_far(k_, n - 1)

    def own_at(i):
        return pl.ds(pl.multiple_of(t * frames + i * CHUNK, CHUNK), CHUNK)

    def total_of(k_, i):
        at = pl.ds(pl.multiple_of(i * CHUNK, CHUNK), CHUNK)
        return (
            parts[k_, own_at(i), :].astype(F32)
            + near_in[k_, 0, at, :].astype(F32)
            + far_in[k_, at, :].astype(F32)
        )

    def stage(k_, i, value, dst):
        few = CHUNK // 2
        staged[k_, pl.ds(i * few, few)] = value.reshape(few, 2, -1).astype(BF16)

        def send_one(peer, carry):
            @pl.when(peer != tm)
            def _():
                remote(
                    staged.at[k_, peer], dst.at[0, tm], back_send.at[k_], back_recv.at[k_], tm=peer
                ).start()

            return carry

        lax.fori_loop(i * few, (i + 1) * few, send_one, 0)

    def keep_own(k_, dst):
        pltpu.make_async_copy(staged.at[k_, tm], dst.at[0, tm], back_recv.at[k_]).start()

    def await_parts(k_):
        await_bytes(near_in.at[k_, 0], near_recv.at[k_])
        await_bytes(far_in.at[k_], far_recv.at[k_])

    n_columns = width // heads_width
    def mix(n, carry):
        at = pl.ds(pl.multiple_of(n * heads_width, heads_width), heads_width)
        parts[0, :, at] = nt(att[...], w[3, at, :]).astype(BF16)
        chunk_done(0, n)
        return carry

    lax.fori_loop(0, width // heads_width, mix, 0)
    forward(1)
    await_bytes(rows_all.at[1, pl.ds(0, 2 * frames)], spread_near.at[1])
    d_att[...] = nn(rows_all[1], w[3]).astype(BF16)
    to_far(0, n_columns - 1)

    def attend_back(p, carry):
        at = pl.ds(pl.multiple_of(p * pair, pair), pair)
        for h in range(heads):
            cols = slice(h * HEAD_DIM, (h + 1) * HEAD_DIM)
            qh, kh, vh, doh = q[at, cols], k[at, cols], v[at, cols], d_att[at, cols]
            prob = probs[p * heads + h]
            delta = jnp.sum(doh.astype(F32) * att[at, cols].astype(F32), axis=1, keepdims=True)
            d_score = (prob * (nt(doh, vh) - delta)).astype(BF16)
            grads[0, at, cols] = (nn(d_score, kh) * scale).astype(BF16)
            grads[1, at, cols] = (tn(d_score, qh) * scale).astype(BF16)
            grads[2, at, cols] = tn(prob.astype(BF16), doh).astype(BF16)
        return carry

    lax.fori_loop(0, rows // pair, attend_back, 0)
    d_low = jnp.concatenate((nt(grads[0], up[0]), nt(grads[2], up[1])), axis=1).astype(BF16)
    up_part[0:rank] = tn(low[:, 0:rank], grads[0])
    up_part[rank:] = tn(low[:, rank:], grads[2])

    for n in range(n_columns):
        down_part[n] = tn(d_low, normed[:, n * heads_width : (n + 1) * heads_width])
    down_in[t] = down_part[t]
    for d in range(1, n_tensor):
        peer = (t + d) % n_tensor
        remote(down_part.at[peer], down_in.at[t], down_send, down_recv, tensor=peer).start()

    def finish_out(i, carry):
        stage(0, i, rows_all[0, own_at(i), :].astype(F32) + total_of(0, i), out_back)
        return carry

    def outward(n, carry):
        at = pl.ds(pl.multiple_of(n * heads_width, heads_width), heads_width)
        parts[1, :, at] = (
            nt(grads[0], w[0, at, :])
            + nt(grads[1], w[1, at, :])
            + nt(grads[2], w[2, at, :])
            + nn(d_low[:, 0:rank], down[0, :, at])
            + nn(d_low[:, rank:], down[1, :, at])
        ).astype(BF16)
        chunk_done(1, n)

        @pl.when(n == n_columns - 2)
        def _():
            await_parts(0)
            lax.fori_loop(0, frames // CHUNK, finish_out, 0)
            keep_own(0, out_back)

        return carry

    lax.fori_loop(0, width // heads_width, outward, 0)
    to_far(1, n_columns - 1)
    def to_group(pick, dst, stage_):
        def one(d, carry):
            peer = (r + d) % n_group
            remote(
                pick(peer), dst.at[r], g_send.at[stage_], g_recv.at[stage_],
                dp=peer // n_half, tm=(peer % n_half) * Z + z,
            ).start()
            return carry

        lax.fori_loop(1, n_group, one, 0)

    await_bytes(down_in.at[pl.ds(0, n_tensor - 1)], down_recv)
    n_rows = part.shape[1]
    for a in range(n_group // 2):
        part[a] = jnp.sum(down_in[:, a * n_rows : (a + 1) * n_rows, :], axis=0)
        part[n_group // 2 + a] = up_part[a * n_rows : (a + 1) * n_rows, :]
    to_group(lambda peer: part.at[peer], first, 0)
    first[r] = part[r]
    await_bytes(first.at[pl.ds(0, n_group - 1)], g_recv.at[0])
    sent_sum[0] = jnp.sum(first[...], axis=0).astype(BF16)

    def along_z(stage_, slot, peer_of):
        for d in range(1, 4):
            remote(
                sent_sum.at[stage_], fours.at[stage_, slot], z_send_sum.at[stage_], z_recv_sum.at[stage_],
                tm=yh * Z + peer_of(d),
            ).start()
        fours[stage_, slot] = sent_sum[stage_]

    along_z(0, z % 4, lambda d: z // 4 * 4 + (z + d) % 4)
    await_parts(1)
    await_bytes(fours.at[0, pl.ds(0, 3)], z_recv_sum.at[0])
    sent_sum[1] = jnp.sum(fours[0].astype(F32), axis=0).astype(BF16)
    along_z(1, z // 4, lambda d: (z + 4 * d) % Z)

    def finish_grad(i, carry):
        xhat, rstd = standardize(rows_all[0, own_at(i), :])
        g = total_of(1, i) * gain[...]
        m1 = jnp.mean(g, axis=-1, keepdims=True)
        m2 = jnp.mean(g * xhat, axis=-1, keepdims=True)
        stage(1, i, rows_all[1, own_at(i), :].astype(F32) + rstd * (g - m1 - xhat * m2), grad_back)
        return carry

    lax.fori_loop(0, frames // CHUNK, finish_grad, 0)
    keep_own(1, grad_back)
    await_bytes(fours.at[1, pl.ds(0, 3)], z_recv_sum.at[1])
    wide_sum[0] = jnp.sum(fours[1].astype(F32), axis=0)
    total[r] = wide_sum[0]
    to_group(lambda peer: wide_sum.at[0], total, 2)
    await_bytes(total.at[pl.ds(0, n_group - 1)], g_recv.at[2])
    lower = pl.ds(0, n_group // 2)
    for d in range(1, n_tensor):
        remote(
            total.at[lower], down_all.at[t], g_send.at[3], g_recv.at[3], tensor=(t + d) % n_tensor
        ).start()
    down_all[t] = total[lower]
    await_bytes(down_all.at[pl.ds(0, n_tensor - 1)], g_recv.at[3])
    per_map = n_group // 4
    for a in range(n_group // 2):
        at = slice(a % per_map * n_rows, (a % per_map + 1) * n_rows)
        grad_up[a // per_map, at, :] = total[n_group // 2 + a]
        for tensor in range(n_tensor):
            grad_down[a // per_map, at, tensor * heads_width : (tensor + 1) * heads_width] = down_all[tensor, a]

    await_bytes(sq.at[pl.ds(0, n_tensor - 1)], sq_send)
    await_bytes(column.at[pl.ds(0, n_tm - 1)], column_send)
    for k_ in range(2):
        await_bytes(landed.at[k_, pl.ds(0, n_tm - 1)], swap_send.at[k_])
        await_bytes(rows_all.at[k_, pl.ds(0, 3 * frames)], spread_send.at[k_])
        await_bytes(far_in.at[k_], far_send.at[k_])
        await_bytes(w.at[0], x_send.at[k_])
    await_bytes(w.at[0, pl.ds(0, (Z + 1) * depth)], y_send)
    for j in range(3):
        await_bytes(w.at[0, pl.ds(0, Z // 2 * depth)], z_send.at[0])
        await_bytes(w.at[0, pl.ds(0, (Z // 2 - 1) * depth)], z_send.at[1])
    await_bytes(near_in, near_send)
    await_bytes(down_in.at[pl.ds(0, n_tensor - 1)], down_send)
    await_bytes(first.at[pl.ds(0, n_group - 1)], g_send.at[0])
    for stage_ in range(2):
        await_bytes(fours.at[stage_, pl.ds(0, 3)], z_send_sum.at[stage_])
    await_bytes(first.at[pl.ds(0, n_group - 1)], g_send.at[2])
    await_bytes(down_all.at[pl.ds(0, n_tensor - 1)], g_send.at[3])
    for k_, dst in ((0, out_back), (1, grad_back)):
        await_bytes(dst.at[0], back_recv.at[k_])
        await_bytes(staged.at[k_, pl.ds(0, n_tm - 1)], back_send.at[k_])


def fused(tok, cot, qkv, out_t, gain, down, up, codes, offsets, sizes):
    n_dp, n_tm, n_tensor = sizes
    patches, few, width = tok.shape
    frames = patches * few
    rows = n_tensor * frames
    rank, heads_width = up.shape[1:]
    n_group = n_dp * n_tm // Z
    chunk = (4 * rank // n_group, heads_width)
    pair = 2 * frames

    def bf16(*shape):
        return pltpu.VMEM(shape, BF16)

    def f32(*shape):
        return pltpu.VMEM(shape, F32)

    act = bf16(rows, heads_width)
    same = jax.ShapeDtypeStruct((1,) + tok.shape, BF16)
    return pl.pallas_call(
        functools.partial(fused_kernel, n_dp, n_tm, n_tensor, frames),
        out_shape=(
            same,
            same,
            jax.ShapeDtypeStruct((2, rank, width), F32),
            jax.ShapeDtypeStruct(up.shape, F32),
        ),
        in_specs=[SMEM, SMEM, ANY, ANY] + [VMEM] * 5,
        out_specs=(ANY, ANY, VMEM, VMEM),
        scratch_shapes=[
            f32(n_group, *chunk),
            f32(n_tensor, n_group // 2, *chunk),
            bf16(4, qkv.shape[1], heads_width),
            f32(n_tensor, out_t.shape[0], 128),
            f32(n_tm, 2, heads_width),
            bf16(2, *tok.shape),
            bf16(2, rows, width),
            bf16(4, width, heads_width),
            bf16(rows, width),
            act, act, act, act, act,
            bf16(3, rows, heads_width),
            bf16(rows, 2 * rank),
            f32(rows // pair * (heads_width // HEAD_DIM), pair, pair),
            bf16(2, rows, width),
            bf16(2, 2, frames, width),
            bf16(2, frames, width),
            bf16(2, frames, width),
            bf16(2, *tok.shape),
            f32(width // heads_width, 2 * rank, heads_width),
            f32(2 * rank, heads_width),
            f32(n_tensor, 2 * rank, heads_width),
            f32(n_group, *chunk),
            f32(n_group, *chunk),
            bf16(2, 4, *chunk),
            f32(1, *chunk),
            bf16(2, *chunk),
            DMA, DMA, DMA, DMA, DMA((2,)), DMA((2,)), DMA((2,)), DMA((2,)), DMA((2,)),
            DMA((2,)), DMA((2, Z // 2, 3)), DMA, DMA, DMA, DMA((2,)), DMA((2,)), DMA,
            DMA, DMA((2, width // heads_width)), DMA((2,)), DMA((2,)), DMA((2,)), DMA, DMA, DMA((2,)), DMA((2,)), DMA((4,)), DMA((4,)), DMA((2,)), DMA((2,)),
        ],
        compiler_params=pltpu.CompilerParams(
            collective_id=0, has_side_effects=True, vmem_limit_bytes=56 << 20
        ),
    )(codes, offsets, tok, cot, qkv, out_t, gain.reshape(1, width), down.transpose(0, 2, 1), up)


def on_device(tokens, gain, qkv, out, down, up, codes, offsets, cotangent):
    sizes = tuple(lax.axis_size(a) for a in ("dp", "tm", "tensor"))
    block_out, grad_tokens, grad_down, grad_up = fused(
        tokens[0], cotangent[0], qkv, out.T, gain, down, up, codes, offsets, sizes
    )
    return block_out, grad_tokens, grad_down.transpose(0, 2, 1), grad_up


def solution(mesh):
    return jax.shard_map(
        on_device,
        mesh=mesh,
        in_specs=(
            P("dp", "tensor", "tm", None),
            P(),
            P(None, "tm", "tensor"),
            P("tensor", "tm"),
            P(),
            P(None, None, "tensor"),
            P(),
            P("dp"),
            P("dp", "tensor", "tm", None),
        ),
        out_specs=(
            P("dp", "tensor", "tm", None),
            P("dp", "tensor", "tm", None),
            P(),
            P(None, None, "tensor"),
        ),
        check_vma=False,
    )
```

```python
import functools

import jax
import jax.numpy as jnp
from jax import lax
from jax.experimental import pallas as pl
from jax.experimental.pallas import tpu as pltpu
from jax.sharding import PartitionSpec as P

MESH = pl.DeviceIdType.MESH
ANY = pl.BlockSpec(memory_space=pl.ANY)
VMEM = pl.BlockSpec(memory_space=pltpu.VMEM)
SMEM = pl.BlockSpec(memory_space=pltpu.SMEM)
DMA = pltpu.SemaphoreType.DMA
Z = 16
CHUNK = 16

HEAD_DIM = 128
F32 = jnp.float32
BF16 = jnp.bfloat16


def standardize(rows):
    wide = rows.astype(F32)
    removed = wide - jnp.mean(wide, axis=-1, keepdims=True)
    rstd = lax.rsqrt(jnp.mean(removed * removed, axis=-1, keepdims=True) + 1e-05)
    return removed * rstd, rstd


def remote(src, dst, send, recv, **where):
    return pltpu.make_async_remote_copy(
        src_ref=src, dst_ref=dst, send_sem=send, recv_sem=recv, device_id=where, device_id_type=MESH
    )


def await_bytes(ref, sem):
    pltpu.make_async_copy(ref, ref, sem).wait()


def nn(a, b):
    return jnp.dot(a, b, preferred_element_type=F32)


def nt(a, b):
    return lax.dot_general(a, b, (((1,), (1,)), ((), ())), preferred_element_type=F32)


def tn(a, b):
    return lax.dot_general(a, b, (((0,), (0,)), ((), ())), preferred_element_type=F32)


def fused_kernel(
    n_dp, n_tm, n_tensor, frames, codes, offsets, tok, cot, qkv, out_t, gain, down, up,
    out_back, grad_back, grad_down, grad_up,
    total, down_all, shard, sq, column, landed, rows_all, w, normed, q, k, v, att, d_att, grads, low, probs,
    parts, near_in, far_out, far_in, staged, down_part, up_part, down_in, part, first, fours, wide_sum, sent_sum,
    column_send, column_recv, sq_send, sq_recv, swap_send, swap_recv, spread_send, spread_far, spread_near,
    z_send, z_recv, y_send, y_first, y_recv, x_send, x_recv, local,
    near_send, near_first, near_recv, far_send, far_recv, down_send, down_recv, back_send, back_recv, g_send, g_recv, z_send_sum, z_recv_sum,
):
    x, tm, t = lax.axis_index("dp"), lax.axis_index("tm"), lax.axis_index("tensor")
    z, yh = tm % Z, tm // Z
    up_z = yh * Z + (z + 1) % Z
    down_z = yh * Z + (z + Z - 1) % Z
    other = (tm + Z) % n_tm
    near = t + 1 - 2 * (t % 2)
    far = (t + 2) % n_tensor
    near_far = (near + 2) % n_tensor
    mats = (x, (x + 2) % n_dp)
    n_half = n_tm // Z
    n_group = n_dp * n_half
    r = x * n_half + yh
    depth = qkv.shape[1]
    rows, width = normed.shape
    heads_width = q.shape[1]
    rank = up.shape[1]

    def block_of(tensor):
        return pl.ds(pl.multiple_of(tensor * frames, frames), frames)

    def piece_of(half, zs):
        return pl.ds(pl.multiple_of((half * Z + zs) * depth, depth), depth)

    def half_of(half):
        return pl.ds(pl.multiple_of(half * Z * depth, Z * depth), Z * depth)

    barrier = pltpu.get_barrier_semaphore()
    greeted = 0
    for count, address in (
        (n_tm - 1, lambda d: {"tm": (tm + d) % n_tm}),
        (n_tensor - 1, lambda d: {"tensor": (t + d) % n_tensor}),
        (n_dp - 1, lambda d: {"dp": (x + d) % n_dp}),
        (n_dp - 1, lambda d: {"dp": (x + d) % n_dp, "tm": other}),
    ):

        def greet(d, carry, address=address):
            pl.semaphore_signal(barrier, inc=1, device_id=address(d), device_id_type=MESH)
            return carry

        lax.fori_loop(1, count + 1, greet, 0)
        greeted += count
    wide = out_t[...].astype(F32)
    sq[t] = jnp.broadcast_to(jnp.sum(wide * wide, axis=1, keepdims=True), sq.shape[1:])
    for j in range(3):
        shard[j] = qkv[j]
    shard[3] = out_t[...]
    for i in range(2):
        block = shard[mats[i]].astype(F32)
        column[tm, i : i + 1, :] = jnp.sum(block * block, axis=0, keepdims=True)
    pl.semaphore_wait(barrier, greeted)

    def send_column(d, carry):
        peer = (tm + d) % n_tm
        remote(column.at[tm], column.at[tm], column_send, column_recv, tm=peer).start()
        return carry

    lax.fori_loop(1, n_tm, send_column, 0)
    for d in range(1, n_tensor):
        remote(sq.at[t], sq.at[t], sq_send, sq_recv, tensor=(t + d) % n_tensor).start()

    sources = (tok, cot)
    for k_ in range(2):
        pltpu.make_async_copy(sources[k_].at[tm], landed.at[k_, tm], swap_recv.at[k_]).start()

    def swap(first_, last):
        for k_ in range(2):

            def send_one(d, carry, k_=k_):
                peer = (tm + d) % n_tm
                remote(
                    sources[k_].at[peer], landed.at[k_, tm], swap_send.at[k_], swap_recv.at[k_], tm=peer
                ).start()
                return carry

            least = k_ * (n_tm - 1)
            low_, high_ = (jnp.clip(at - least, 0, n_tm - 1) for at in (first_, last))
            lax.fori_loop(1 + low_, 1 + high_, send_one, 0)

    swap(0, 31)
    await_bytes(sq.at[pl.ds(0, n_tensor - 1)], sq_recv)
    mean_out = jnp.sum(sq[...], axis=0)[:, 0:1] / (n_tensor * out_t.shape[1])
    bound_out = (1.0 + codes[3].astype(F32)) * jnp.sqrt(mean_out + 1e-06)
    await_bytes(column.at[pl.ds(0, n_tm - 1)], column_recv)
    mean_in = jnp.sum(column[...], axis=0) / width
    for i, m in enumerate(mats):

        def clip_columns(i=i, m=m):
            bound = (1.0 + codes[m].astype(F32)) * jnp.sqrt(mean_in[i : i + 1] + 1e-06)
            shard[m] = (bound * jnp.tanh(shard[m].astype(F32) / bound)).astype(BF16)

        def clip_rows():
            shard[3] = (bound_out * jnp.tanh(wide / bound_out)).astype(BF16)

        pl.when(m != 3)(clip_columns)
        pl.when(m == 3)(clip_rows)

    def to_z(src, i, piece, half, zs, step, up_side):
        side = 0 if up_side else 1
        remote(
            src, w.at[mats[i], piece_of(half, zs)], z_send.at[side], z_recv.at[side, step, piece],
            tm=up_z if up_side else down_z,
        ).start()

    def to_x(src, half, zs):
        for side, dest in ((0, (x + 1) % n_dp), (1, (x + n_dp - 1) % n_dp)):
            remote(src, w.at[x, piece_of(half, zs)], x_send.at[side], x_recv.at[side], dp=dest).start()

    def to_y(src, zs):
        remote(src, w.at[mats[1], piece_of(yh, zs)], y_send, y_recv, tm=other).start()

    remote(shard.at[x], w.at[x, piece_of(yh, z)], y_send, y_first, tm=other).start()
    for i in range(2):
        to_z(shard.at[mats[i]], i, i, yh, z, 0, True)
        to_z(shard.at[mats[i]], i, i, yh, z, 0, False)
    to_x(shard.at[x], yh, z)
    to_y(shard.at[mats[1]], z)
    for i in range(2):
        pltpu.make_async_copy(shard.at[mats[i]], w.at[mats[i], piece_of(yh, z)], local).start()
    here = w.at[x, piece_of(1 - yh, z)]
    await_bytes(here, y_first)
    to_z(here, 0, 2, 1 - yh, z, 0, True)
    to_z(here, 0, 2, 1 - yh, z, 0, False)
    to_x(here, 1 - yh, z)

    def arrive(step, up_side, onward):
        zs = (z + Z - 1 - step) % Z if up_side else (z + 1 + step) % Z
        side = 0 if up_side else 1
        for piece, (i, half) in enumerate(((0, yh), (1, yh), (0, 1 - yh))):
            here = w.at[mats[i], piece_of(half, zs)]
            await_bytes(here, z_recv.at[side, step, piece])
            if onward:
                to_z(here, i, piece, half, zs, step + 1, up_side)
            if i == 0:
                to_x(here, half, zs)
            else:
                to_y(here, zs)

    def ring(step, carry):
        arrive(step, True, True)
        arrive(step, False, True)
        swap(31 + step * 10, 31 + (step + 1) * 10)
        return carry

    def spread(k_):
        await_bytes(landed.at[k_], swap_recv.at[k_])
        for i in range(frames // CHUNK):
            pairs = landed[k_, i * CHUNK // 2 : (i + 1) * CHUNK // 2].astype(F32)
            at = pl.ds(pl.multiple_of(t * frames + i * CHUNK, CHUNK), CHUNK)
            rows_all[k_, at, :] = pairs.reshape(CHUNK, -1).astype(BF16)
        mine = rows_all.at[k_, block_of(t)]
        remote(mine, mine, spread_send.at[k_], spread_far.at[k_], tensor=far).start()
        remote(mine, mine, spread_send.at[k_], spread_near.at[k_], tensor=near).start()

    def forward(k_):
        mine = rows_all.at[k_, block_of(far)]
        await_bytes(mine, spread_far.at[k_])
        remote(mine, mine, spread_send.at[k_], spread_near.at[k_], tensor=near).start()

    lax.fori_loop(0, 5, ring, 0)
    spread(0)
    lax.fori_loop(5, Z // 2 - 2, ring, 0)
    swap(31 + (Z // 2 - 2) * 10, 2 * (n_tm - 1))
    arrive(Z // 2 - 2, True, True)
    arrive(Z // 2 - 2, False, False)
    arrive(Z // 2 - 1, True, False)
    spread(1)
    forward(0)
    await_bytes(rows_all.at[0, pl.ds(0, 2 * frames)], spread_near.at[0])

    def norm(p, carry):
        at = pl.ds(pl.multiple_of(p * 32, 32), 32)
        xhat, _ = standardize(rows_all[0, at, :])
        normed[at, :] = (xhat * gain[...].reshape(1, width)).astype(BF16)
        return carry

    lax.fori_loop(0, rows // 32, norm, 0)
    for i in range(2):
        low[:, i * rank : (i + 1) * rank] = nt(normed[...], down[i]).astype(BF16)

    await_bytes(shard.at[pl.ds(0, 2)], local)
    await_bytes(w.at[mats[1], half_of(1 - yh)], y_recv)
    await_bytes(w.at[(x + n_dp - 1) % n_dp], x_recv.at[0])
    await_bytes(w.at[(x + 1) % n_dp], x_recv.at[1])
    q[...] = (nn(normed[...], w[0]) + nn(low[:, 0:rank], up[0])).astype(BF16)
    k[...] = nn(normed[...], w[1]).astype(BF16)
    v[...] = (nn(normed[...], w[2]) + nn(low[:, rank:], up[1])).astype(BF16)

    pair = 2 * frames
    heads = heads_width // HEAD_DIM
    scale = HEAD_DIM ** (-0.5)
    t_at = lax.broadcasted_iota(jnp.int32, (pair, pair), 0)
    s_at = lax.broadcasted_iota(jnp.int32, (pair, pair), 1)
    allowed = (s_at <= t_at + offsets[0]) & (s_at // frames == t_at // frames)

    def attend(p, carry):
        at = pl.ds(pl.multiple_of(p * pair, pair), pair)
        for h in range(heads):
            cols = slice(h * HEAD_DIM, (h + 1) * HEAD_DIM)
            masked = jnp.where(allowed, nt(q[at, cols], k[at, cols]) * scale, -1e30)
            expo = jnp.exp(masked - jnp.max(masked, axis=1, keepdims=True))
            prob = expo / jnp.sum(expo, axis=1, keepdims=True)
            probs[p * heads + h] = prob
            att[at, cols] = nn(prob.astype(BF16), v[at, cols]).astype(BF16)
        return carry

    lax.fori_loop(0, rows // pair, attend, 0)

    def columns(n):
        return pl.ds(pl.multiple_of(n * heads_width, heads_width), heads_width)

    def to_near(k_, n):
        for i, tensor, sem in ((1, near_far, near_first.at[k_, n]), (0, near, near_recv.at[k_])):
            remote(
                parts.at[k_, block_of(tensor), columns(n)], near_in.at[k_, i, :, columns(n)], near_send, sem,
                tensor=near,
            ).start()

    def to_far(k_, n):
        at = columns(n)
        await_bytes(near_in.at[k_, 1, :, at], near_first.at[k_, n])
        far_out[k_, :, at] = (
            parts[k_, block_of(far), at].astype(F32) + near_in[k_, 1, :, at].astype(F32)
        ).astype(BF16)
        remote(
            far_out.at[k_, :, at], far_in.at[k_, :, at], far_send.at[k_], far_recv.at[k_], tensor=far
        ).start()

    def chunk_done(k_, n):
        to_near(k_, n)

        @pl.when(n > 0)
        def _():
            to_far(k_, n - 1)

    def own_at(i):
        return pl.ds(pl.multiple_of(t * frames + i * CHUNK, CHUNK), CHUNK)

    def total_of(k_, i):
        at = pl.ds(pl.multiple_of(i * CHUNK, CHUNK), CHUNK)
        return (
            parts[k_, own_at(i), :].astype(F32)
            + near_in[k_, 0, at, :].astype(F32)
            + far_in[k_, at, :].astype(F32)
        )

    def stage(k_, i, value, dst):
        few = CHUNK // 2
        staged[k_, pl.ds(i * few, few)] = value.reshape(few, 2, -1).astype(BF16)

        def send_one(peer, carry):
            @pl.when(peer != tm)
            def _():
                remote(
                    staged.at[k_, peer], dst.at[0, tm], back_send.at[k_], back_recv.at[k_], tm=peer
                ).start()

            return carry

        lax.fori_loop(i * few, (i + 1) * few, send_one, 0)

    def keep_own(k_, dst):
        pltpu.make_async_copy(staged.at[k_, tm], dst.at[0, tm], back_recv.at[k_]).start()

    def await_parts(k_):
        await_bytes(near_in.at[k_, 0], near_recv.at[k_])
        await_bytes(far_in.at[k_], far_recv.at[k_])

    n_columns = width // heads_width
    def mix(n, carry):
        at = pl.ds(pl.multiple_of(n * heads_width, heads_width), heads_width)
        parts[0, :, at] = nt(att[...], w[3, at, :]).astype(BF16)
        chunk_done(0, n)
        return carry

    lax.fori_loop(0, width // heads_width, mix, 0)
    forward(1)
    await_bytes(rows_all.at[1, pl.ds(0, 2 * frames)], spread_near.at[1])
    d_att[...] = nn(rows_all[1], w[3]).astype(BF16)
    to_far(0, n_columns - 1)

    def attend_back(p, carry):
        at = pl.ds(pl.multiple_of(p * pair, pair), pair)
        for h in range(heads):
            cols = slice(h * HEAD_DIM, (h + 1) * HEAD_DIM)
            qh, kh, vh, doh = q[at, cols], k[at, cols], v[at, cols], d_att[at, cols]
            prob = probs[p * heads + h]
            delta = jnp.sum(doh.astype(F32) * att[at, cols].astype(F32), axis=1, keepdims=True)
            d_score = (prob * (nt(doh, vh) - delta)).astype(BF16)
            grads[0, at, cols] = (nn(d_score, kh) * scale).astype(BF16)
            grads[1, at, cols] = (tn(d_score, qh) * scale).astype(BF16)
            grads[2, at, cols] = tn(prob.astype(BF16), doh).astype(BF16)
        return carry

    lax.fori_loop(0, rows // pair, attend_back, 0)
    d_low = jnp.concatenate((nt(grads[0], up[0]), nt(grads[2], up[1])), axis=1).astype(BF16)
    up_part[0:rank] = tn(low[:, 0:rank], grads[0])
    up_part[rank:] = tn(low[:, rank:], grads[2])

    for n in range(n_columns):
        down_part[n] = tn(d_low, normed[:, n * heads_width : (n + 1) * heads_width])
    down_in[t] = down_part[t]
    for d in range(1, n_tensor):
        peer = (t + d) % n_tensor
        remote(down_part.at[peer], down_in.at[t], down_send, down_recv, tensor=peer).start()

    def finish_out(i, carry):
        stage(0, i, rows_all[0, own_at(i), :].astype(F32) + total_of(0, i), out_back)
        return carry

    def outward(n, carry):
        at = pl.ds(pl.multiple_of(n * heads_width, heads_width), heads_width)
        parts[1, :, at] = (
            nt(grads[0], w[0, at, :])
            + nt(grads[1], w[1, at, :])
            + nt(grads[2], w[2, at, :])
            + nn(d_low[:, 0:rank], down[0, :, at])
            + nn(d_low[:, rank:], down[1, :, at])
        ).astype(BF16)
        chunk_done(1, n)

        @pl.when(n == n_columns - 2)
        def _():
            await_parts(0)
            lax.fori_loop(0, frames // CHUNK, finish_out, 0)
            keep_own(0, out_back)

        return carry

    lax.fori_loop(0, width // heads_width, outward, 0)
    to_far(1, n_columns - 1)
    def to_group(pick, dst, stage_):
        def one(d, carry):
            peer = (r + d) % n_group
            remote(
                pick(peer), dst.at[r], g_send.at[stage_], g_recv.at[stage_],
                dp=peer // n_half, tm=(peer % n_half) * Z + z,
            ).start()
            return carry

        lax.fori_loop(1, n_group, one, 0)

    await_bytes(down_in.at[pl.ds(0, n_tensor - 1)], down_recv)
    n_rows = part.shape[1]
    for a in range(n_group // 2):
        part[a] = jnp.sum(down_in[:, a * n_rows : (a + 1) * n_rows, :], axis=0)
        part[n_group // 2 + a] = up_part[a * n_rows : (a + 1) * n_rows, :]
    to_group(lambda peer: part.at[peer], first, 0)
    first[r] = part[r]
    await_bytes(first.at[pl.ds(0, n_group - 1)], g_recv.at[0])
    sent_sum[0] = jnp.sum(first[...], axis=0).astype(BF16)

    def along_z(stage_, slot, peer_of):
        for d in range(1, 4):
            remote(
                sent_sum.at[stage_], fours.at[stage_, slot], z_send_sum.at[stage_], z_recv_sum.at[stage_],
                tm=yh * Z + peer_of(d),
            ).start()
        fours[stage_, slot] = sent_sum[stage_]

    along_z(0, z % 4, lambda d: z // 4 * 4 + (z + d) % 4)
    await_parts(1)
    await_bytes(fours.at[0, pl.ds(0, 3)], z_recv_sum.at[0])
    sent_sum[1] = jnp.sum(fours[0].astype(F32), axis=0).astype(BF16)
    along_z(1, z // 4, lambda d: (z + 4 * d) % Z)

    def finish_grad(i, carry):
        xhat, rstd = standardize(rows_all[0, own_at(i), :])
        g = total_of(1, i) * gain[...].reshape(1, width)
        m1 = jnp.mean(g, axis=-1, keepdims=True)
        m2 = jnp.mean(g * xhat, axis=-1, keepdims=True)
        stage(1, i, rows_all[1, own_at(i), :].astype(F32) + rstd * (g - m1 - xhat * m2), grad_back)
        return carry

    lax.fori_loop(0, frames // CHUNK, finish_grad, 0)
    keep_own(1, grad_back)
    await_bytes(fours.at[1, pl.ds(0, 3)], z_recv_sum.at[1])
    wide_sum[0] = jnp.sum(fours[1].astype(F32), axis=0)
    total[r] = wide_sum[0]
    to_group(lambda peer: wide_sum.at[0], total, 2)
    await_bytes(total.at[pl.ds(0, n_group - 1)], g_recv.at[2])
    lower = pl.ds(0, n_group // 2)
    for d in range(1, n_tensor):
        remote(
            total.at[lower], down_all.at[t], g_send.at[3], g_recv.at[3], tensor=(t + d) % n_tensor
        ).start()
    down_all[t] = total[lower]
    await_bytes(down_all.at[pl.ds(0, n_tensor - 1)], g_recv.at[3])
    per_map = n_group // 4
    for a in range(n_group // 2):
        at = slice(a % per_map * n_rows, (a % per_map + 1) * n_rows)
        grad_up[a // per_map, at, :] = total[n_group // 2 + a]
        for tensor in range(n_tensor):
            grad_down[a // per_map, at, tensor * heads_width : (tensor + 1) * heads_width] = down_all[tensor, a]

    await_bytes(sq.at[pl.ds(0, n_tensor - 1)], sq_send)
    await_bytes(column.at[pl.ds(0, n_tm - 1)], column_send)
    for k_ in range(2):
        await_bytes(landed.at[k_, pl.ds(0, n_tm - 1)], swap_send.at[k_])
        await_bytes(rows_all.at[k_, pl.ds(0, 3 * frames)], spread_send.at[k_])
        await_bytes(far_in.at[k_], far_send.at[k_])
        await_bytes(w.at[0], x_send.at[k_])
    await_bytes(w.at[0, pl.ds(0, (Z + 1) * depth)], y_send)
    for j in range(3):
        await_bytes(w.at[0, pl.ds(0, Z // 2 * depth)], z_send.at[0])
        await_bytes(w.at[0, pl.ds(0, (Z // 2 - 1) * depth)], z_send.at[1])
    await_bytes(near_in, near_send)
    await_bytes(down_in.at[pl.ds(0, n_tensor - 1)], down_send)
    await_bytes(first.at[pl.ds(0, n_group - 1)], g_send.at[0])
    for stage_ in range(2):
        await_bytes(fours.at[stage_, pl.ds(0, 3)], z_send_sum.at[stage_])
    await_bytes(first.at[pl.ds(0, n_group - 1)], g_send.at[2])
    await_bytes(down_all.at[pl.ds(0, n_tensor - 1)], g_send.at[3])
    for k_, dst in ((0, out_back), (1, grad_back)):
        await_bytes(dst.at[0], back_recv.at[k_])
        await_bytes(staged.at[k_, pl.ds(0, n_tm - 1)], back_send.at[k_])


def fused(tok, cot, qkv, out_t, gain, down, up, codes, offsets, sizes):
    n_dp, n_tm, n_tensor = sizes
    patches, few, width = tok.shape
    frames = patches * few
    rows = n_tensor * frames
    rank, heads_width = up.shape[1:]
    n_group = n_dp * n_tm // Z
    chunk = (4 * rank // n_group, heads_width)
    pair = 2 * frames

    def bf16(*shape):
        return pltpu.VMEM(shape, BF16)

    def f32(*shape):
        return pltpu.VMEM(shape, F32)

    act = bf16(rows, heads_width)
    same = jax.ShapeDtypeStruct((1,) + tok.shape, BF16)
    return pl.pallas_call(
        functools.partial(fused_kernel, n_dp, n_tm, n_tensor, frames),
        out_shape=(
            same,
            same,
            jax.ShapeDtypeStruct((2, rank, width), F32),
            jax.ShapeDtypeStruct(up.shape, F32),
        ),
        in_specs=[SMEM, SMEM, ANY, ANY] + [VMEM] * 5,
        out_specs=(ANY, ANY, VMEM, VMEM),
        scratch_shapes=[
            f32(n_group, *chunk),
            f32(n_tensor, n_group // 2, *chunk),
            bf16(4, qkv.shape[1], heads_width),
            f32(n_tensor, out_t.shape[0], 128),
            f32(n_tm, 2, heads_width),
            bf16(2, *tok.shape),
            bf16(2, rows, width),
            bf16(4, width, heads_width),
            bf16(rows, width),
            act, act, act, act, act,
            bf16(3, rows, heads_width),
            bf16(rows, 2 * rank),
            f32(rows // pair * (heads_width // HEAD_DIM), pair, pair),
            bf16(2, rows, width),
            bf16(2, 2, frames, width),
            bf16(2, frames, width),
            bf16(2, frames, width),
            bf16(2, *tok.shape),
            f32(width // heads_width, 2 * rank, heads_width),
            f32(2 * rank, heads_width),
            f32(n_tensor, 2 * rank, heads_width),
            f32(n_group, *chunk),
            f32(n_group, *chunk),
            bf16(2, 4, *chunk),
            f32(1, *chunk),
            bf16(2, *chunk),
            DMA, DMA, DMA, DMA, DMA((2,)), DMA((2,)), DMA((2,)), DMA((2,)), DMA((2,)),
            DMA((2,)), DMA((2, Z // 2, 3)), DMA, DMA, DMA, DMA((2,)), DMA((2,)), DMA,
            DMA, DMA((2, width // heads_width)), DMA((2,)), DMA((2,)), DMA((2,)), DMA, DMA, DMA((2,)), DMA((2,)), DMA((4,)), DMA((4,)), DMA((2,)), DMA((2,)),
        ],
        compiler_params=pltpu.CompilerParams(
            collective_id=0, has_side_effects=True, vmem_limit_bytes=56 << 20
        ),
    )(codes, offsets, tok, cot, qkv, out_t, gain, down.transpose(0, 2, 1), up)


def on_device(tokens, gain, qkv, out, down, up, codes, offsets, cotangent):
    sizes = tuple(lax.axis_size(a) for a in ("dp", "tm", "tensor"))
    block_out, grad_tokens, grad_down, grad_up = fused(
        tokens[0], cotangent[0], qkv, out.T, gain, down, up, codes, offsets, sizes
    )
    return block_out, grad_tokens, grad_down.transpose(0, 2, 1), grad_up


def solution(mesh):
    return jax.shard_map(
        on_device,
        mesh=mesh,
        in_specs=(
            P("dp", "tensor", "tm", None),
            P(),
            P(None, "tm", "tensor"),
            P("tensor", "tm"),
            P(),
            P(None, None, "tensor"),
            P(),
            P("dp"),
            P("dp", "tensor", "tm", None),
        ),
        out_specs=(
            P("dp", "tensor", "tm", None),
            P("dp", "tensor", "tm", None),
            P(),
            P(None, None, "tensor"),
        ),
        check_vma=False,
    )
```
